32 devices in a mesh: groups: 2 (over x), lat: 8 (over z, y), lon: 2 (over core).
Axes of the slice: x: 2, y: 2, z: 4, core: 2. Of those that a mesh axis runs over, the one named last changes fastest.
Arguments:
- first_guess: float32 [4, 512, 2048], P(None, ('groups', 'lat'), 'lon'), parts along dimension 1, may hold values from -1.5 to 1.5
- range_coef: float32 [512, 2048], P(('groups', 'lat'), 'lon'), parts along dimension 0, may hold values from 0.5 to 2
- land_sea: int32 [512, 2048], P(('groups', 'lat'), 'lon'), parts along dimension 0, may hold values from 0 to 1
- lat_kernel: float32 [65], replicated, may hold values from 0.001 to 0.06
- lon_kernel: float32 [65], replicated, may hold values from 0.001 to 0.06
- observations: bfloat16 [4, 512, 2048], P('lon', ('groups', 'lat')), parts along dimension 1, may hold values from -6 to 6
- obs_precision: bfloat16 [4, 512, 2048], P('lon', ('groups', 'lat')), parts along dimension 1, may hold values from 1 to 10
- track_counts: int32 [4, 512], P('lon', ('groups', 'lat')), parts along dimension 1, may hold values from 0 to 3
Outputs:
- solution: float32 [4, 512, 2048], P(None, ('groups', 'lat'), 'lon'), parts along dimension 1
- residual: float32 [4, 512, 2048], P(None, ('groups', 'lat'), 'lon'), parts along dimension 1
The draws below stay inside these ranges and needn't reach their ends.
There are 2 independent parts, one for each index of `groups`. The reference program is written for one: setup_inputs(seed, part) draws one part's arguments, and reference() takes and returns one part's arrays. A program takes and returns all parts, laid end to end along the dimension named above; an argument that names none is the same for every part. Nothing has to cross between parts.
All inputs are finite; a program needn't handle non-finite values.
Results may differ from the reference program's by a relative error of at most 0.0003.
Values sent between devices are 32-bit elements; how exact they have to be, the bound alone decides.
No kernel may reach another device: no remote copies, remote signals or barrier semaphores. Data moves between devices by JAX's collectives and lax.ppermute only.
A program may use at most 64 MiB of HBM per device.

```python
import math
import jax
import jax.numpy as jnp
from jax import lax

HALF = 32
ITERS = 2
NDAY = 4
NLAT = 256
NLON = 2048


def wave_sum(lon_wave, lat_freq, lat_phase, lon_phase, amplitude):
    row_index = jnp.arange(NLAT, dtype=jnp.float32)
    col_index = jnp.arange(NLON, dtype=jnp.int32)
    smooth = jnp.zeros((NDAY, NLAT, NLON), jnp.float32)
    for term_index in range(lon_wave.shape[1]):
        lat_angle = 2.0 * math.pi * lat_freq[:, term_index, None] * row_index[None, :] + lat_phase[:, term_index, None]
        cycle = jnp.mod(lon_wave[:, term_index, None] * col_index[None, :], NLON).astype(jnp.float32)
        lon_angle = 2.0 * math.pi * cycle / NLON + lon_phase[:, term_index, None]
        smooth = smooth + amplitude[:, term_index, None, None] * jnp.sin(lat_angle)[:, :, None] * jnp.cos(lon_angle)[:, None, :]
    return smooth


def draw_first_guess(key, part):
    key_wave = jax.random.fold_in(key, 11)
    key_freq = jax.random.fold_in(key, 12)
    key_latphase = jax.random.fold_in(key, 13)
    key_lonphase = jax.random.fold_in(key, 14)
    key_amplitude = jax.random.fold_in(key, 15)
    key_rough = jax.random.fold_in(key, 16)
    key_shortwave = jax.random.fold_in(key, 17)
    key_shortfreq = jax.random.fold_in(key, 18)
    top_wave = max(1, NLON // 256)
    long_wave = jax.random.randint(key_wave, (NDAY, 4), 1, top_wave + 1)
    short_wave = jax.random.randint(key_shortwave, (NDAY, 4), max(1, NLON // 64), NLON // 32 + 1)
    lon_wave = jnp.concatenate([long_wave, short_wave], axis=1)
    long_freq = jax.random.uniform(key_freq, (NDAY, 4), jnp.float32, 1.0 / 1024.0, 1.0 / 256.0)
    short_freq = jax.random.uniform(key_shortfreq, (NDAY, 4), jnp.float32, 1.0 / 64.0, 1.0 / 32.0)
    lat_freq = jnp.concatenate([long_freq, short_freq], axis=1)
    lat_phase = jax.random.uniform(key_latphase, (NDAY, 8), jnp.float32, 0.0, 2.0 * math.pi)
    lon_phase = jax.random.uniform(key_lonphase, (NDAY, 8), jnp.float32, 0.0, 2.0 * math.pi)
    amplitude = jax.random.uniform(key_amplitude, (NDAY, 8), jnp.float32, 0.08, 0.2)
    smooth = wave_sum(lon_wave, lat_freq, lat_phase, lon_phase, amplitude)
    rough_part = jnp.clip(0.05 * jax.random.normal(key_rough, (NDAY, NLAT, NLON), jnp.float32), -0.2, 0.2)
    total = smooth + rough_part
    return jnp.clip(total, -1.5, 1.5).astype(jnp.float32)


def draw_land_sea(key, part):
    key_coarse = jax.random.fold_in(key, 21)
    key_jitter = jax.random.fold_in(key, 22)
    coarse_rows = NLAT // 32 + 2
    coarse_cols = NLON // 32 + 2
    coarse = jax.random.randint(key_coarse, (coarse_rows, coarse_cols), 0, 100)
    fine = jnp.repeat(jnp.repeat(coarse, 32, axis=0), 32, axis=1)
    level = fine[:NLAT, :NLON] + fine[16:NLAT + 16, :NLON]
    level = level + fine[:NLAT, 16:NLON + 16] + fine[16:NLAT + 16, 16:NLON + 16]
    level = level + jax.random.randint(key_jitter, (NLAT, NLON), 0, 40)
    return (level >= 187).astype(jnp.int32)


def with_ends(array, key, low, high):
    longest = array.shape.index(max(array.shape))
    spots = []
    for shift in (0, 1):
        where = [jax.random.randint(jax.random.fold_in(key, axis), (), 0, length) for axis, length in enumerate(array.shape)]
        where[longest] = (where[longest] + shift) % array.shape[longest]
        spots.append(tuple(where))
    return array.at[spots[0]].set(low).at[spots[1]].set(high)


def steps_of(own_key, dims, cuts, low, largest):
    def one(axis_at, parts):
        steps = jax.random.uniform(jax.random.fold_in(jax.random.fold_in(own_key, 6), axis_at), (parts,), jnp.float32, low / len(cuts), largest / len(cuts))
        return jnp.repeat(jnp.exp(steps), dims[axis_at] // parts).reshape((-1,) + (1,) * (len(dims) - axis_at - 1))

    factor_of = one(*cuts[0])
    for cut in cuts[1:]:
        factor_of = factor_of * one(*cut)
    return factor_of


def noise(rng, dims, spread, most, pieces=(), held_as=jnp.bfloat16):
    array = spread * jax.random.normal(rng, dims, jnp.float32)
    if pieces:
        array = array * steps_of(rng, dims, pieces, -0.22, 0.18)
    return jnp.clip(array, -most, most).astype(held_as)


def setup_inputs(seed: int = 0, part: int = 0) -> dict:
    key_list = jax.random.split(jax.random.key(seed), 9)
    own_keys = jax.random.split(jax.random.fold_in(key_list[8], part), 9)
    first_guess = draw_first_guess(jax.random.fold_in(jax.random.fold_in(key_list[8], part), 71), part)
    range_coef = jnp.clip(jnp.exp(math.log(2.0) - 1.3862944 * jax.random.uniform(own_keys[1], (NLAT, NLON), jnp.float32) ** steps_of(own_keys[1], (NLAT, NLON), ((0, 8), (1, 2)), -0.2, 0.2)), 0.5, 2.0)
    land_sea = draw_land_sea(jax.random.fold_in(jax.random.fold_in(key_list[8], part), 71), part)
    lat_kernel = jnp.clip(jnp.exp(jax.random.uniform(key_list[3], (2 * HALF + 1,), jnp.float32, math.log(0.001), math.log(0.06))), 0.001, 0.06)
    lon_kernel = jnp.clip(jnp.exp(jax.random.uniform(key_list[4], (2 * HALF + 1,), jnp.float32, math.log(0.001), math.log(0.06))), 0.001, 0.06)
    observations = noise(own_keys[5], (NDAY, NLAT, NLON), 1.0, 6.0, ((0, 2), (1, 8)))
    obs_precision = jnp.clip(jnp.exp(math.log(10.0) - 2.3025851 * jax.random.uniform(own_keys[6], (NDAY, NLAT, NLON), jnp.float32) ** steps_of(own_keys[6], (NDAY, NLAT, NLON), ((0, 2), (1, 8)), -0.2, 0.2)), 1.0, 10.0).astype(jnp.bfloat16)
    track_counts = with_ends(jax.random.randint(own_keys[7], (NDAY, NLAT), 0, 4), jax.random.fold_in(own_keys[7], 1), 0, 3).astype(jnp.int32)
    return dict(first_guess=first_guess, range_coef=range_coef, land_sea=land_sea, lat_kernel=lat_kernel, lon_kernel=lon_kernel, observations=observations, obs_precision=obs_precision, track_counts=track_counts)


LOWER = 0.25
UPPER = 120.0


def conv_lat(field, kern):
    out = lax.conv_general_dilated(field[:, None], kern.reshape(1, 1, -1, 1), (1, 1), ((HALF, HALF), (0, 0)), precision=lax.Precision.HIGHEST)
    return out[:, 0]


def conv_lon(field, kern):
    wrapped = jnp.pad(field, ((0, 0), (0, 0), (HALF, HALF)), mode="wrap")
    out = lax.conv_general_dilated(wrapped[:, None], kern.reshape(1, 1, 1, -1), (1, 1), ((0, 0), (0, 0)), precision=lax.Precision.HIGHEST)
    return out[:, 0]


def apply_a(field, coef):
    padded = jnp.pad(field, ((0, 0), (1, 1), (0, 0)))
    beside = padded[:, 2:, :] + padded[:, :-2, :]
    beside = beside + jnp.roll(field, 1, axis=2) + jnp.roll(field, -1, axis=2)
    return (coef[None] + 4.0) * field - beside


def reference(first_guess, range_coef, land_sea, lat_kernel, lon_kernel, observations, obs_precision, track_counts):
    sea = land_sea.astype(jnp.float32)[None]
    weight = track_counts.astype(jnp.float32)[:, :, None] * obs_precision.astype(jnp.float32)
    obs = observations.astype(jnp.float32)

    def resid(state):
        masked = sea * state
        seen = conv_lon(conv_lat(masked, lat_kernel), lon_kernel)
        misfit = weight * (obs - seen)
        back = conv_lat(conv_lon(misfit, lon_kernel[::-1]), lat_kernel[::-1])
        prior = apply_a(apply_a(masked, range_coef), range_coef)
        return sea * back - sea * prior - (1.0 - sea) * state

    theta = (LOWER + UPPER) / 2.0
    delta = (UPPER - LOWER) / 2.0
    sigma = theta / delta
    rho = 1.0 / sigma
    state = first_guess
    update = jnp.zeros_like(first_guess)
    last = first_guess
    for step in range(ITERS):
        last = resid(state)
        if step == 0:
            update = last / theta
        else:
            new_rho = 1.0 / (2.0 * sigma - rho)
            update = new_rho * rho * update + (2.0 * new_rho / delta) * last
            rho = new_rho
        state = state + update
    return state, last
```

```python
import functools

import jax
import jax.numpy as jnp
from jax import lax
from jax.experimental import pallas as pl
from jax.experimental.pallas import tpu as pltpu
from jax.sharding import PartitionSpec as P

HALF = 32
TAPS = 2 * HALF + 1
LOWER = 0.25
UPPER = 120.0
THETA = (LOWER + UPPER) / 2.0
DELTA = (UPPER - LOWER) / 2.0
SIGMA = THETA / DELTA
RHO = 1.0 / SIGMA
NEW_RHO = 1.0 / (2.0 * SIGMA - RHO)
BLOCK = 256
EDGE = 128
AXES = ("lat", "lon")

VMEM = pl.BlockSpec(memory_space=pltpu.VMEM)
SMEM = pl.BlockSpec(memory_space=pltpu.SMEM)
F32 = jnp.float32
BF16 = jnp.bfloat16


def place():
    lat = lax.axis_index("lat")
    return lat // 2, lax.rem(lat, 2), lax.axis_index("lon")


def shape(*dims, dtype=F32):
    return jax.ShapeDtypeStruct(dims, dtype)


def call(kernel, out_shape, args, specs=None, scratch=(), flops=0, name=None):
    nbytes = sum(a.size * a.dtype.itemsize for a in args)
    nbytes += sum(o.size * o.dtype.itemsize for o in out_shape)
    return pl.pallas_call(
        kernel,
        out_shape=out_shape,
        in_specs=specs or [VMEM] * len(args),
        out_specs=[VMEM] * len(out_shape),
        scratch_shapes=list(scratch),
        compiler_params=pltpu.CompilerParams(vmem_limit_bytes=24 * 2**20),
        cost_estimate=pl.CostEstimate(flops=flops, bytes_accessed=nbytes, transcendentals=0),
        name=name,
    )(*args)


def pack_kernel(guess_ref, land_ref, own_ref, core_ref, pair_ref, diag_ref):
    _, y, c = place()
    sea = land_ref[...].astype(F32)
    own_ref[...] = guess_ref[2 * c + y] * sea
    core_ref[...] = guess_ref[2 * (1 - c) + y] * sea
    pair_ref[...] = guess_ref[2 * c + (1 - y)] * sea
    diag_ref[...] = guess_ref[2 * (1 - c) + (1 - y)] * sea


def obs_kernel(obs_ref, precision_ref, counts_ref, keep_ref, send_ref):
    _, y, c = place()
    width = obs_ref.shape[2] // 2
    for day, ref in ((y, keep_ref), (1 - y, send_ref)):
        counts = counts_ref[day].astype(F32)
        for half, side in ((0, c), (1, 1 - c)):
            source = pl.ds(pl.multiple_of(side * width, width), width)
            target = pl.ds(half * width, width)
            ref[0, :, target] = obs_ref[day, :, source].astype(F32)
            ref[1, :, target] = counts * precision_ref[day, :, source].astype(F32)


def split(values):
    high = values.astype(BF16)
    return high, (values - high.astype(F32)).astype(BF16)


def banded(kern_ref, offset):
    forward = jnp.zeros(offset.shape, F32)
    adjoint = jnp.zeros(offset.shape, F32)
    for tap in range(TAPS):
        hit = offset == tap
        forward = jnp.where(hit, kern_ref[tap], forward)
        adjoint = jnp.where(hit, kern_ref[TAPS - 1 - tap], adjoint)
    return forward, adjoint


def matrix_kernel(rows, lat_ref, lon_ref, lat_fwd_ref, lat_adj_ref, lon_fwd_ref, lon_adj_ref):
    _, y, _ = place()
    dims = (2 * rows, 4 * rows)

    def where_row(block, inside):
        return rows * jnp.where(y == 0, block, 1 - block) + inside

    out = lax.broadcasted_iota(jnp.int32, dims, 0)
    col = lax.broadcasted_iota(jnp.int32, dims, 1)
    offset = where_row(col // rows - 1, col % rows) - where_row(out // rows, out % rows) + HALF
    for ref, matrix in zip((lat_fwd_ref, lat_adj_ref), banded(lat_ref, offset)):
        high, low = split(matrix)
        ref[: 2 * rows, : 4 * rows] = high
        ref[: 2 * rows, 4 * rows :] = high
        ref[2 * rows :, : 4 * rows] = low
        ref[2 * rows :, 4 * rows :] = jnp.zeros(dims, BF16)
    dims = (EDGE, EDGE)
    offset = lax.broadcasted_iota(jnp.int32, dims, 0) - lax.broadcasted_iota(jnp.int32, dims, 1)
    for ref in (lon_fwd_ref, lon_adj_ref):
        ref[...] = jnp.zeros(ref.shape, BF16)
    for distance in range(3):
        pair = banded(lon_ref, offset + EDGE * distance - (EDGE - HALF))
        for ref, matrix in zip((lon_fwd_ref, lon_adj_ref), pair):
            for part, piece in enumerate(split(matrix)):
                for column in range(BLOCK // EDGE):
                    row = EDGE * (column + distance)
                    ref[part, row : row + EDGE, EDGE * column : EDGE * (column + 1)] = piece


def coef_kernel(own_ref, core_ref, pair_ref, diag_ref, coef_ref, sea_ref, first_ref, second_ref):
    _, y, _ = place()
    rows, width = own_ref.shape[1:]
    own = jnp.concatenate([own_ref[0], core_ref[0]], axis=1) + 4.0
    pair = jnp.concatenate([pair_ref[0], diag_ref[0]], axis=1) + 4.0
    coef_ref[pl.ds(pl.multiple_of(rows * y, rows), rows), :] = own
    coef_ref[pl.ds(pl.multiple_of(rows * (1 - y), rows), rows), :] = pair
    sea_ref[:rows, :width] = own_ref[1]
    sea_ref[:rows, width:] = core_ref[1]
    sea_ref[rows:, :width] = pair_ref[1]
    sea_ref[rows:, width:] = diag_ref[1]
    first_ref[...] = jnp.where(y == 0, own[:8], own[rows - 8 :])
    second_ref[...] = jnp.where(y == 0, pair[rows - 8 :], pair[:8])


def load(refs):
    if len(refs) == 1:
        return refs[0][...]
    return jnp.concatenate([ref[...] for ref in refs], axis=1)


def lat_conv(blocks, matrix_ref):
    high, low = split(jnp.concatenate(blocks, axis=0))
    stacked = jnp.concatenate([high, low], axis=0)
    both = jnp.dot(matrix_ref[...], stacked, preferred_element_type=F32)
    half = both.shape[0] // 2
    return both[:half] + both[half:]


def lon_conv(field, matrix_ref):
    rows, length = field.shape
    count = length // BLOCK
    parts = []
    for part in split(field):
        wide = jnp.concatenate([part[:, -EDGE:], part, part[:, :EDGE]], axis=1)
        parts += [wide[:, BLOCK * i : BLOCK * (i + 1) + 2 * EDGE] for i in range(count)]
    coarse = jnp.dot(jnp.concatenate(parts, axis=0), matrix_ref[0], preferred_element_type=F32)
    fine = jnp.dot(
        jnp.concatenate(parts[:count], axis=0), matrix_ref[1], preferred_element_type=F32
    )
    out = coarse[: count * rows] + coarse[count * rows :] + fine
    return jnp.concatenate([out[rows * i : rows * (i + 1)] for i in range(count)], axis=1)


def misfit_kernel(halves, *refs):
    fields = [load(refs[halves * i : halves * (i + 1)]) for i in range(4)]
    keep_ref, sent_ref, lat_ref, fwd_ref, adj_ref, own_ref, pair_ref = refs[4 * halves :]
    seen = lon_conv(lat_conv(fields, lat_ref), fwd_ref)
    obs = jnp.concatenate([keep_ref[0], sent_ref[0]], axis=0)
    weight = jnp.concatenate([keep_ref[1], sent_ref[1]], axis=0)
    back = lon_conv(weight * (obs - seen), adj_ref)
    rows = own_ref.shape[0]
    own_ref[...] = back[:rows]
    pair_ref[...] = back[rows:]


def beside(center, above, below):
    width = center.shape[1]
    lateral = pltpu.roll(center, 1, 1) + pltpu.roll(center, width - 1, 1)
    return above + below + lateral


def prior_kernel(pairs, halves, *refs):
    second, own, pair, first = [load(refs[halves * i : halves * (i + 1)]) for i in range(4)]
    coef_ref, sea_ref, second_ref, first_ref, out_ref, ext, wide, inner = refs[4 * halves :]
    k, y, _ = place()
    rows, length = own.shape
    for where, values in (
        (jnp.where(y == 0, 0, 3), second),
        (jnp.where(y == 0, 1, 2), own),
        (jnp.where(y == 0, 2, 1), pair),
        (jnp.where(y == 0, 3, 0), first),
    ):
        ext[pl.ds(pl.multiple_of(rows * where, rows), rows), :] = values
    coef = coef_ref[...]
    wide[8 : 8 + 2 * rows, :] = coef
    wide[:8, :] = jnp.where(y == 0, second_ref[...], first_ref[...])
    wide[8 + 2 * rows :, :] = jnp.where(y == 0, first_ref[...], second_ref[...])
    low, count = rows - 8, 2 * rows + 16
    center = ext[low : low + count, :]
    around = beside(center, ext[low - 1 : low - 1 + count, :], ext[low + 1 : low + 1 + count, :])
    inner[...] = wide[...] * center - around
    north = jnp.where(k == 0, 0.0, 1.0)
    south = jnp.where(k == pairs - 1, 0.0, 1.0)
    inner[:8, :] = inner[:8, :] * north
    inner[8 + 2 * rows :, :] = inner[8 + 2 * rows :, :] * south
    center = inner[8 : 8 + 2 * rows, :]
    outer = coef * center - beside(center, inner[7 : 7 + 2 * rows, :], inner[9 : 9 + 2 * rows, :])
    ext[: 2 * rows, :] = outer
    out_ref[:rows, :] = ext[pl.ds(pl.multiple_of(rows * y, rows), rows), :]
    out_ref[rows:, :] = ext[pl.ds(pl.multiple_of(rows * (1 - y), rows), rows), :]
    out_ref[...] = out_ref[...] * sea_ref[...]


def update_kernel(halves, *refs):
    second, own, pair, first = [ref[...] for ref in refs[:4]]
    lat_ref, prior_ref, sea_ref = refs[4:7]
    back = lat_conv([second, own, pair, first], lat_ref)
    last = sea_ref[...] * back - prior_ref[...]
    rows, length = own.shape
    width = length // 2
    outs = refs[7 + 2 * halves :]
    outs[0][...] = last[:rows, :width]
    outs[1][...] = last[:rows, width:]
    outs[2][...] = last[rows:, :width]
    outs[3][...] = last[rows:, width:]
    if halves:
        outs[4][...] = load(refs[7 : 7 + halves]) + last[:rows] * (1.0 / THETA)
        outs[5][...] = load(refs[7 + halves : 7 + 2 * halves]) + last[rows:] * (1.0 / THETA)


def final_kernel(*refs):
    early, late = refs[:4], refs[4:8]
    guess_ref, land_ref, state_ref, last_ref = refs[8:]
    _, y, c = place()
    land = 1.0 - land_ref[...].astype(F32)
    days = (2 * c + y, 2 * (1 - c) + y, 2 * c + (1 - y), 2 * (1 - c) + (1 - y))
    for day, early_ref, late_ref in zip(days, early, late):
        guess = guess_ref[day]
        update = (early_ref[...] - land * guess) * (1.0 / THETA)
        state = guess + update
        last = late_ref[...] - land * state
        update = (NEW_RHO * RHO) * update + (2.0 * NEW_RHO / DELTA) * last
        state_ref[day] = state + update
        last_ref[day] = last


def body(
    pairs,
    first_guess,
    range_coef,
    land_sea,
    lat_kernel,
    lon_kernel,
    observations,
    obs_precision,
    track_counts,
):
    days, rows, width = first_guess.shape
    length = observations.shape[2]
    assert days == 4 and rows == HALF and length == 2 * width and length % BLOCK == 0
    places = [(k, y, c) for k in range(pairs) for y in range(2) for c in range(2)]

    def permute(array, move):
        number = {at: i for i, at in enumerate(places)}
        moves = [(number[at], number[move(*at)]) for at in places if move(*at) in number]
        return lax.ppermute(array, AXES, moves)

    core = lambda array: permute(array, lambda k, y, c: (k, y, 1 - c))
    pair = lambda array: permute(array, lambda k, y, c: (k, 1 - y, c))
    diag = lambda array: permute(array, lambda k, y, c: (k, 1 - y, 1 - c))
    first = lambda array: permute(array, lambda k, y, c: (k + 2 * y - 1, y, c))
    second = lambda array: permute(array, lambda k, y, c: (k + 1 - 2 * y, y, c))

    piece = shape(rows, width)
    band = shape(rows, length)
    own, to_core, to_pair, to_diag = call(
        pack_kernel, [piece] * 4, [first_guess, land_sea], name="pack"
    )
    by_pair, by_diag, by_core = pair(to_pair), diag(to_diag), core(to_core)
    keep, send = call(
        obs_kernel,
        [shape(2, rows, length)] * 2,
        [observations, obs_precision, track_counts[:, :, None]],
        name="observed",
    )
    lat_fwd, lat_adj, lon_fwd, lon_adj = call(
        functools.partial(matrix_kernel, rows),
        [shape(4 * rows, 8 * rows, dtype=BF16)] * 2
        + [shape(2, BLOCK + 2 * EDGE, BLOCK, dtype=BF16)] * 2,
        [lat_kernel, lon_kernel],
        [SMEM, SMEM],
        flops=4 * 65 * 2 * 70000,
        name="matrices",
    )
    maps = jnp.stack([range_coef, land_sea.astype(F32)])

    send, by_pair, by_diag = lax.optimization_barrier((send, by_pair, by_diag))
    v_first = [first(own), first(by_core)]
    v_second = [second(by_pair), second(by_diag)]
    sent = pair(send)
    maps, sent = lax.optimization_barrier((maps, sent))
    maps_pair = pair(maps)
    maps_core = core(maps)
    maps_diag = core(maps_pair)
    coef, sea, edge_first, edge_second = call(
        coef_kernel,
        [shape(2 * rows, length)] * 2 + [shape(8, length)] * 2,
        [maps, maps_core, maps_pair, maps_diag],
        name="maps",
    )
    edge_first, edge_second = first(edge_first), second(edge_second)

    v_own, v_pair = [own, by_core], [by_pair, by_diag]
    pieces = []
    conv = 2 * 3 * 2 * rows * length * 512
    for step in range(2):
        halves = len(v_own)
        fields = v_second + v_own + v_pair + v_first
        m_own, m_pair = call(
            functools.partial(misfit_kernel, halves),
            [band] * 2,
            fields + [keep, sent, lat_fwd, lon_fwd, lon_adj],
            flops=3 * conv,
            name="misfit",
        )
        m_first, m_second = first(m_own), second(m_pair)
        (prior,) = call(
            functools.partial(prior_kernel, pairs, halves),
            [shape(2 * rows, length)],
            fields + [coef, sea, edge_second, edge_first],
            scratch=[
                pltpu.VMEM((4 * rows, length), F32),
                pltpu.VMEM((2 * rows + 16, length), F32),
                pltpu.VMEM((2 * rows + 16, length), F32),
            ],
            flops=20 * 2 * rows * length,
            name="prior",
        )
        base = v_own + v_pair if step == 0 else []
        outs = call(
            functools.partial(update_kernel, len(base) // 2),
            [piece] * 4 + ([band] * 2 if base else []),
            [m_second, m_own, m_pair, m_first, lat_adj, prior, sea] + base,
            flops=conv,
            name="update",
        )
        pieces += [outs[0], core(outs[1]), pair(outs[2]), diag(outs[3])]
        if base:
            v_own, v_pair = [outs[4]], [outs[5]]
            v_first, v_second = [first(outs[4])], [second(outs[5])]
    state, last = call(
        final_kernel,
        [shape(days, rows, width)] * 2,
        pieces + [first_guess, land_sea],
        name="final",
    )
    return state, last


def solution(mesh):
    assert mesh.shape["lat"] % 2 == 0 and mesh.shape["lon"] == 2
    in_specs = (
        P(None, ("groups", "lat"), "lon"),
        P(("groups", "lat"), "lon"),
        P(("groups", "lat"), "lon"),
        P(),
        P(),
        P("lon", ("groups", "lat"), None),
        P("lon", ("groups", "lat"), None),
        P("lon", ("groups", "lat")),
    )
    out_specs = (P(None, ("groups", "lat"), "lon"), P(None, ("groups", "lat"), "lon"))
    return jax.shard_map(
        functools.partial(body, mesh.shape["lat"] // 2),
        mesh=mesh,
        in_specs=in_specs,
        out_specs=out_specs,
        check_vma=False,
    )
```

```python
import functools

import jax
import jax.numpy as jnp
from jax import lax
from jax.experimental import pallas as pl
from jax.experimental.pallas import tpu as pltpu
from jax.sharding import PartitionSpec as P

HALF = 32
TAPS = 2 * HALF + 1
LOWER = 0.25
UPPER = 120.0
THETA = (LOWER + UPPER) / 2.0
DELTA = (UPPER - LOWER) / 2.0
SIGMA = THETA / DELTA
RHO = 1.0 / SIGMA
NEW_RHO = 1.0 / (2.0 * SIGMA - RHO)
BLOCK = 256
EDGE = 128
ADJOINT_COST = 2 * 10**10
PACK_VMEM = 62 * 2**20
AXES = ("lat", "lon")

VMEM = pl.BlockSpec(memory_space=pltpu.VMEM)
SMEM = pl.BlockSpec(memory_space=pltpu.SMEM)
HBM = pl.BlockSpec(memory_space=pltpu.HBM)
F32 = jnp.float32
BF16 = jnp.bfloat16


def place():
    lat = lax.axis_index("lat")
    return lat // 2, lax.rem(lat, 2), lax.axis_index("lon")


def open_sides(pairs):
    k, _, _ = place()
    north, south = jnp.where(k == 0, 0.0, 1.0), jnp.where(k == pairs - 1, 0.0, 1.0)
    even = lax.rem(k, 2) == 0
    return jnp.where(even, north, south), jnp.where(even, south, north)


def odd_even(own, pair):
    k, y, _ = place()
    straight = lax.rem(k + y, 2) == 0
    return jnp.where(straight, own, pair), jnp.where(straight, pair, own)


def shape(*dims, dtype=F32):
    return jax.ShapeDtypeStruct(dims, dtype)


def call(
    kernel, out_shape, args, specs=None, outs=None, scratch=(), flops=0, vmem=24 * 2**20, name=None
):
    nbytes = sum(a.size * a.dtype.itemsize for a in args)
    nbytes += sum(o.size * o.dtype.itemsize for o in out_shape)
    return pl.pallas_call(
        kernel,
        out_shape=out_shape,
        in_specs=specs or [VMEM] * len(args),
        out_specs=outs or [VMEM] * len(out_shape),
        scratch_shapes=list(scratch),
        compiler_params=pltpu.CompilerParams(vmem_limit_bytes=vmem),
        cost_estimate=pl.CostEstimate(flops=flops, bytes_accessed=nbytes, transcendentals=0),
        name=name,
    )(*args)


def pack_kernel(guess_ref, land_ref, coef_ref, own_ref, core_ref, pair_ref, diag_ref, *scratch):
    guess, land, coef, packed, sems = scratch
    _, y, c = place()
    days = (2 * c + (1 - y), 2 * (1 - c) + (1 - y), 2 * (1 - c) + y, 2 * c + y)
    rows, width = land.shape
    start = pl.multiple_of((rows - 8) * y, 8)
    copies = [
        pltpu.make_async_copy(land_ref, land, sems.at[0]),
        pltpu.make_async_copy(coef_ref.at[pl.ds(start, 8), :], coef, sems.at[1]),
    ]
    for i, day in enumerate(days):
        copies.append(pltpu.make_async_copy(guess_ref.at[day], guess.at[i], sems.at[2 + i]))
    for copy in copies:
        copy.start()
    copies[0].wait()
    copies[1].wait()
    edge = jnp.where(y == 0, coef[:1, :], coef[7:, :])
    edge = jnp.concatenate([edge[:, i : i + 128] for i in range(0, width, 128)], axis=0)
    outs = []
    for i, ref in enumerate((pair_ref, diag_ref, core_ref, own_ref)):
        copies[2 + i].wait()
        for group in range(rows // 8):
            part = slice(8 * group, 8 * group + 8)
            sea = land[part, :].astype(F32)
            packed[i, :, width * group : width * (group + 1)] = guess[i, part, :] * sea
        packed[i, :, width * (rows // 8) :] = edge
        outs.append(pltpu.make_async_copy(packed.at[i], ref, sems.at[6 + i]))
        outs[-1].start()
    for out in outs:
        out.wait()


def order_kernel(own_ref, core_ref, pair_ref, diag_ref, odd_ref, even_ref):
    size = own_ref.shape[1]
    for i, (own, pair) in enumerate(((own_ref, pair_ref), (core_ref, diag_ref))):
        odd, even = odd_even(own[...], pair[...])
        odd_ref[:, size * i : size * (i + 1)] = odd
        even_ref[:, size * i : size * (i + 1)] = even


def obs_kernel(obs_ref, precision_ref, counts_ref, keep_ref, send_ref):
    _, y, c = place()
    width = obs_ref.shape[2] // 2
    for day, ref in ((y, keep_ref), (1 - y, send_ref)):
        counts = counts_ref[day].astype(F32)
        for half, side in ((0, c), (1, 1 - c)):
            source = pl.ds(pl.multiple_of(side * width, width), width)
            target = pl.ds(half * width, width)
            ref[0, :, target] = obs_ref[day, :, source].astype(F32)
            ref[1, :, target] = counts * precision_ref[day, :, source].astype(F32)


def split(values):
    high = values.astype(BF16)
    return high, (values - high.astype(F32)).astype(BF16)


def banded(kern_ref, offset):
    forward = jnp.zeros(offset.shape, F32)
    adjoint = jnp.zeros(offset.shape, F32)
    for tap in range(TAPS):
        hit = offset == tap
        forward = jnp.where(hit, kern_ref[tap], forward)
        adjoint = jnp.where(hit, kern_ref[TAPS - 1 - tap], adjoint)
    return forward, adjoint


def matrix_kernel(pairs, rows, lat_ref, lon_ref, lat_fwd_ref, lat_adj_ref, lon_fwd_ref, lon_adj_ref):
    k, y, _ = place()
    dims = (2 * rows, 4 * rows)

    even = lax.rem(k, 2) == 0
    out = lax.broadcasted_iota(jnp.int32, dims, 0)
    col = lax.broadcasted_iota(jnp.int32, dims, 1)
    target = rows * jnp.where(y == 0, out // rows, 1 - out // rows) + out % rows
    source = rows * jnp.where(even, col // rows - 1, 2 - col // rows) + col % rows
    offset = source - target + HALF
    odd_open, even_open = open_sides(pairs)
    inside = jnp.where(col < 3 * rows, 1.0, even_open)
    inside = jnp.where(col < rows, odd_open, inside)
    for ref, matrix in zip((lat_fwd_ref, lat_adj_ref), banded(lat_ref, offset)):
        high, low = split(matrix * inside)
        ref[: 2 * rows, : 4 * rows] = high
        ref[: 2 * rows, 4 * rows :] = high
        ref[2 * rows :, : 4 * rows] = low
        ref[2 * rows :, 4 * rows :] = jnp.zeros(dims, BF16)
    dims = (EDGE, EDGE)
    offset = lax.broadcasted_iota(jnp.int32, dims, 0) - lax.broadcasted_iota(jnp.int32, dims, 1)
    for ref in (lon_fwd_ref, lon_adj_ref):
        ref[...] = jnp.zeros(ref.shape, BF16)
    for distance in range(3):
        pair = banded(lon_ref, offset + EDGE * distance - (EDGE - HALF))
        for ref, matrix in zip((lon_fwd_ref, lon_adj_ref), pair):
            for part, piece in enumerate(split(matrix)):
                for column in range(BLOCK // EDGE):
                    row = EDGE * (column + distance)
                    ref[part, row : row + EDGE, EDGE * column : EDGE * (column + 1)] = piece


def load(ref):
    if ref.shape[0] > 8:
        return ref[...]
    size, groups = ref.shape[1] // 2, HALF // 8
    width = (size - 128) // groups
    return jnp.concatenate(
        [
            jnp.concatenate(
                [ref[:, size * half + width * i : size * half + width * (i + 1)] for half in range(2)],
                axis=1,
            )
            for i in range(groups)
        ],
        axis=0,
    )


def edge_row(ref):
    size = ref.shape[1] // 2
    tiles = [ref[:, size * half - 128 : size * half] for half in (1, 2)]
    return jnp.concatenate([tile[i : i + 1, :] for tile in tiles for i in range(8)], axis=1)


def lat_conv(blocks, matrix_ref):
    high, low = split(jnp.concatenate(blocks, axis=0))
    stacked = jnp.concatenate([high, low], axis=0)
    both = jnp.dot(matrix_ref[...], stacked, preferred_element_type=F32)
    half = both.shape[0] // 2
    return both[:half] + both[half:]


def lon_conv(field, matrix_ref):
    rows, length = field.shape
    count = length // BLOCK
    parts = []
    for part in split(field):
        wide = jnp.concatenate([part[:, -EDGE:], part, part[:, :EDGE]], axis=1)
        parts += [wide[:, BLOCK * i : BLOCK * (i + 1) + 2 * EDGE] for i in range(count)]
    coarse = jnp.dot(jnp.concatenate(parts, axis=0), matrix_ref[0], preferred_element_type=F32)
    fine = jnp.dot(
        jnp.concatenate(parts[:count], axis=0), matrix_ref[1], preferred_element_type=F32
    )
    out = coarse[: count * rows] + coarse[count * rows :] + fine
    return jnp.concatenate([out[rows * i : rows * (i + 1)] for i in range(count)], axis=1)


def seen_kernel(*refs):
    fields = [load(ref) for ref in refs[:4]]
    lat_ref, fwd_ref, seen_ref = refs[4:]
    seen_ref[...] = lon_conv(lat_conv(fields, lat_ref), fwd_ref)


def misfit_kernel(seen_ref, keep_ref, sent_ref, adj_ref, odd_ref, even_ref):
    obs = jnp.concatenate([keep_ref[0], sent_ref[0]], axis=0)
    weight = jnp.concatenate([keep_ref[1], sent_ref[1]], axis=0)
    spread = lon_conv(weight * (obs - seen_ref[...]), adj_ref)
    rows = odd_ref.shape[0]
    odd_ref[...], even_ref[...] = odd_even(spread[:rows], spread[rows:])


def beside(center, above, below):
    width = center.shape[1]
    lateral = pltpu.roll(center, 1, 1) + pltpu.roll(center, width - 1, 1)
    return above + below + lateral


def prior_kernel(pairs, *refs):
    fields = [load(ref) for ref in refs[:4]]
    odd_edge, even_edge = edge_row(refs[4]), edge_row(refs[5])
    map_refs = refs[6:10]
    out_ref, ext, wide, inner = refs[10:]
    k, y, _ = place()
    rows, length = fields[0].shape
    even = lax.rem(k, 2) == 0
    odd_open, even_open = open_sides(pairs)
    fields[0] = fields[0] * odd_open
    fields[3] = fields[3] * even_open
    for block, field in enumerate(fields):
        where = rows * jnp.where(even, block, 3 - block)
        ext[pl.ds(pl.multiple_of(where, rows), rows), :] = field
    for block, (left, right) in enumerate((map_refs[:2], map_refs[2:])):
        where = pl.multiple_of(8 + rows * jnp.where(y == 0, block, 1 - block), 8)
        coef = jnp.concatenate([left[0], right[0]], axis=1) + 4.0
        wide[pl.ds(where, rows), :] = coef
    north = jnp.where(even, odd_edge, even_edge) + 4.0
    south = jnp.where(even, even_edge, odd_edge) + 4.0
    wide[:8, :] = jnp.broadcast_to(north, (8, length))
    wide[8 + 2 * rows :, :] = jnp.broadcast_to(south, (8, length))
    low, count = rows - 8, 2 * rows + 16
    center = ext[low : low + count, :]
    around = beside(center, ext[low - 1 : low - 1 + count, :], ext[low + 1 : low + 1 + count, :])
    inner[...] = wide[...] * center - around
    inner[:8, :] = inner[:8, :] * jnp.where(k == 0, 0.0, 1.0)
    inner[8 + 2 * rows :, :] = inner[8 + 2 * rows :, :] * jnp.where(k == pairs - 1, 0.0, 1.0)
    center = inner[8 : 8 + 2 * rows, :]
    around = beside(center, inner[7 : 7 + 2 * rows, :], inner[9 : 9 + 2 * rows, :])
    ext[: 2 * rows, :] = wide[8 : 8 + 2 * rows, :] * center - around
    out_ref[:rows, :] = ext[pl.ds(pl.multiple_of(rows * y, rows), rows), :]
    out_ref[rows:, :] = ext[pl.ds(pl.multiple_of(rows * (1 - y), rows), rows), :]


def adjoint_kernel(*refs):
    refs[5][...] = lat_conv([ref[...] for ref in refs[:4]], refs[4])


def update_kernel(final, *refs):
    back_ref, prior_ref, left, right, pair_left, pair_right = refs[:6]
    last = back_ref[...] - prior_ref[...]
    rows, length = last.shape[0] // 2, last.shape[1]
    width = length // 2
    last_own = last[:rows] * jnp.concatenate([left[1], right[1]], axis=1)
    last_pair = last[rows:] * jnp.concatenate([pair_left[1], pair_right[1]], axis=1)
    outs = refs[-4:] if final else refs[-6:]
    outs[0][...] = last_own[:, :width]
    outs[1][...] = last_own[:, width:]
    outs[2][...] = last_pair[:, :width]
    outs[3][...] = last_pair[:, width:]
    if not final:
        odd, even = odd_even(last_own, last_pair)
        outs[4][...] = load(refs[6]) + odd * (1.0 / THETA)
        outs[5][...] = load(refs[7]) + even * (1.0 / THETA)


def final_kernel(*refs):
    early, late = refs[:4], refs[4:8]
    guess_ref, land_ref, state_ref, last_ref = refs[8:]
    _, y, c = place()
    land = 1.0 - land_ref[...].astype(F32)
    days = (2 * c + y, 2 * (1 - c) + y, 2 * c + (1 - y), 2 * (1 - c) + (1 - y))
    for day, early_ref, late_ref in zip(days, early, late):
        guess = guess_ref[day]
        update = (early_ref[...] - land * guess) * (1.0 / THETA)
        state = guess + update
        last = late_ref[...] - land * state
        update = (NEW_RHO * RHO) * update + (2.0 * NEW_RHO / DELTA) * last
        state_ref[day] = state + update
        last_ref[day] = last


def body(
    pairs,
    first_guess,
    range_coef,
    land_sea,
    lat_kernel,
    lon_kernel,
    observations,
    obs_precision,
    track_counts,
):
    days, rows, width = first_guess.shape
    length = observations.shape[2]
    assert days == 4 and rows == HALF and length == 2 * width and length % BLOCK == 0
    assert width == 8 * 128
    places = [(k, y, c) for k in range(pairs) for y in range(2) for c in range(2)]

    def permute(array, move):
        moves = [(i, places.index(move(*at))) for i, at in enumerate(places)]
        return lax.ppermute(array, AXES, moves)

    def swap(k, y, c, parity):
        target = k + 1 if k % 2 == parity else k - 1
        return (target, y, c) if 0 <= target < pairs else (k, y, 1 - c)

    core = lambda array: permute(array, lambda k, y, c: (k, y, 1 - c))
    pair = lambda array: permute(array, lambda k, y, c: (k, 1 - y, c))
    diag = lambda array: permute(array, lambda k, y, c: (k, 1 - y, 1 - c))
    odd = lambda array: permute(array, lambda k, y, c: swap(k, y, c, 1))
    even = lambda array: permute(array, lambda k, y, c: swap(k, y, c, 0))

    piece = shape(rows, width)
    packed = shape(8, rows // 8 * width + 128)
    band = shape(rows, length)
    own, to_core, to_pair, to_diag = call(
        pack_kernel,
        [packed] * 4,
        [first_guess, land_sea, range_coef],
        [HBM] * 3,
        scratch=[
            pltpu.VMEM((4, rows, width), F32),
            pltpu.VMEM((rows, width), jnp.int32),
            pltpu.VMEM((8, width), F32),
            pltpu.VMEM((4,) + packed.shape, F32),
            pltpu.SemaphoreType.DMA((10,)),
        ],
        outs=[HBM] * 4,
        vmem=PACK_VMEM,
        name="pack",
    )
    by_pair, by_diag = pair(to_pair), diag(to_diag)
    keep, send = call(
        obs_kernel,
        [shape(2, rows, length)] * 2,
        [observations, obs_precision, track_counts[:, :, None]],
        name="observed",
    )
    lat_fwd, lat_adj, lon_fwd, lon_adj = call(
        functools.partial(matrix_kernel, pairs, rows),
        [shape(4 * rows, 8 * rows, dtype=BF16)] * 2
        + [shape(2, BLOCK + 2 * EDGE, BLOCK, dtype=BF16)] * 2,
        [lat_kernel, lon_kernel],
        [SMEM, SMEM],
        flops=4 * 65 * 2 * 70000,
        name="matrices",
    )
    to_core, lat_fwd = lax.optimization_barrier((to_core, lat_fwd))
    by_core = core(to_core)
    maps = jnp.stack([range_coef, land_sea.astype(F32)])

    send, by_pair, by_diag = lax.optimization_barrier((send, by_pair, by_diag))
    v_odd, v_even = call(
        order_kernel,
        [shape(8, 2 * packed.shape[1])] * 2,
        [own, by_core, by_pair, by_diag],
        name="order",
    )
    fields = [odd(v_odd), v_odd, v_even, even(v_even)]
    edges = [fields[0], fields[3]]
    sent = pair(send)
    conv = 2 * 3 * 2 * rows * length * 512
    maps_core = core(maps)

    pieces = []
    for step in range(2):
        (seen,) = call(
            seen_kernel,
            [shape(2 * rows, length)],
            fields + [lat_fwd, lon_fwd],
            flops=2 * conv,
            name="seen",
        )
        m_odd, m_even = call(
            misfit_kernel, [band] * 2, [seen, keep, sent, lon_adj], flops=conv, name="misfit"
        )
        if not step:
            maps, m_odd, m_even = lax.optimization_barrier((maps, m_odd, m_even))
            maps_pair = pair(maps)
            maps = [maps, maps_core, maps_pair, core(maps_pair)]
        (back,) = call(
            adjoint_kernel,
            [shape(2 * rows, length)],
            [odd(m_odd), m_odd, m_even, even(m_even), lat_adj],
            flops=ADJOINT_COST,
            name="adjoint",
        )
        (prior,) = call(
            functools.partial(prior_kernel, pairs),
            [shape(2 * rows, length)],
            fields + edges + maps,
            scratch=[
                pltpu.VMEM((4 * rows, length), F32),
                pltpu.VMEM((2 * rows + 16, length), F32),
                pltpu.VMEM((2 * rows + 16, length), F32),
            ],
            name="prior",
        )
        outs = call(
            functools.partial(update_kernel, step == 1),
            [piece] * 4 + ([] if step else [band] * 2),
            [back, prior] + maps + ([] if step else [v_odd, v_even]),
            name="update",
        )
        pieces += [outs[0], core(outs[1]), pair(outs[2]), diag(outs[3])]
        if not step:
            fields = [odd(outs[4]), outs[4], outs[5], even(outs[5])]
    state, last = call(
        final_kernel,
        [shape(days, rows, width)] * 2,
        pieces + [first_guess, land_sea],
        name="final",
    )
    return state, last


def solution(mesh):
    assert mesh.shape["lat"] % 2 == 0 and mesh.shape["lon"] == 2
    in_specs = (
        P(None, ("groups", "lat"), "lon"),
        P(("groups", "lat"), "lon"),
        P(("groups", "lat"), "lon"),
        P(),
        P(),
        P("lon", ("groups", "lat"), None),
        P("lon", ("groups", "lat"), None),
        P("lon", ("groups", "lat")),
    )
    out_specs = (P(None, ("groups", "lat"), "lon"), P(None, ("groups", "lat"), "lon"))
    return jax.shard_map(
        functools.partial(body, mesh.shape["lat"] // 2),
        mesh=mesh,
        in_specs=in_specs,
        out_specs=out_specs,
        check_vma=False,
    )
```

```python
import functools

import jax
import jax.numpy as jnp
from jax import lax
from jax.experimental import pallas as pl
from jax.experimental.pallas import tpu as pltpu
from jax.sharding import PartitionSpec as P

HALF = 32
TAPS = 2 * HALF + 1
LOWER = 0.25
UPPER = 120.0
THETA = (LOWER + UPPER) / 2.0
DELTA = (UPPER - LOWER) / 2.0
SIGMA = THETA / DELTA
RHO = 1.0 / SIGMA
NEW_RHO = 1.0 / (2.0 * SIGMA - RHO)
BLOCK = 256
EDGE = 128
LEFT_COST = 5 * 10**9
ADJOINT_COST = 2 * 10**10
PACK_VMEM = 62 * 2**20
AXES = ("lat", "lon")

VMEM = pl.BlockSpec(memory_space=pltpu.VMEM)
SMEM = pl.BlockSpec(memory_space=pltpu.SMEM)
HBM = pl.BlockSpec(memory_space=pltpu.HBM)
F32 = jnp.float32
BF16 = jnp.bfloat16


def place():
    lat = lax.axis_index("lat")
    return lat // 2, lax.rem(lat, 2), lax.axis_index("lon")


def open_sides(pairs):
    k, _, _ = place()
    north, south = jnp.where(k == 0, 0.0, 1.0), jnp.where(k == pairs - 1, 0.0, 1.0)
    even = lax.rem(k, 2) == 0
    return jnp.where(even, north, south), jnp.where(even, south, north)


def odd_even(own, pair):
    k, y, _ = place()
    straight = lax.rem(k + y, 2) == 0
    return jnp.where(straight, own, pair), jnp.where(straight, pair, own)


def shape(*dims, dtype=F32):
    return jax.ShapeDtypeStruct(dims, dtype)


def call(
    kernel, out_shape, args, specs=None, outs=None, scratch=(), flops=0, vmem=24 * 2**20, aliases=None, name=None
):
    nbytes = 0 if flops == 0 else sum(a.size * a.dtype.itemsize for a in args)
    return list(pl.pallas_call(
        kernel,
        out_shape=out_shape,
        in_specs=specs or [VMEM] * len(args),
        out_specs=outs or [VMEM] * len(out_shape),
        scratch_shapes=list(scratch),
        input_output_aliases=aliases or {},
        compiler_params=pltpu.CompilerParams(vmem_limit_bytes=vmem),
        cost_estimate=pl.CostEstimate(flops=flops, bytes_accessed=nbytes, transcendentals=0),
        name=name,
    )(*args))


def pack_kernel(guess_ref, land_ref, coef_ref, own_ref, core_ref, pair_ref, diag_ref, *scratch):
    guess, land, coef, packed, sems = scratch
    _, y, c = place()
    days = (2 * c + (1 - y), 2 * (1 - c) + (1 - y), 2 * (1 - c) + y, 2 * c + y)
    rows, width = land.shape
    start = pl.multiple_of((rows - 8) * y, 8)
    copies = [
        pltpu.make_async_copy(land_ref, land, sems.at[0]),
        pltpu.make_async_copy(coef_ref.at[pl.ds(start, 8), :], coef, sems.at[1]),
    ]
    for i, day in enumerate(days):
        copies.append(pltpu.make_async_copy(guess_ref.at[day], guess.at[i], sems.at[2 + i]))
    for copy in copies:
        copy.start()
    copies[0].wait()
    copies[1].wait()
    edge = jnp.where(y == 0, coef[:1, :], coef[7:, :])
    edge = jnp.concatenate([edge[:, i : i + 128] for i in range(0, width, 128)], axis=0)
    outs = []
    for i, ref in enumerate((pair_ref, diag_ref, core_ref, own_ref)):
        copies[2 + i].wait()
        for group in range(rows // 8):
            part = slice(8 * group, 8 * group + 8)
            sea = land[part, :].astype(F32)
            packed[i, :, width * group : width * (group + 1)] = guess[i, part, :] * sea
        packed[i, :, width * (rows // 8) :] = edge
        outs.append(pltpu.make_async_copy(packed.at[i], ref, sems.at[6 + i]))
        outs[-1].start()
    for out in outs:
        out.wait()


def order_kernel(own_ref, core_ref, pair_ref, diag_ref, odd_ref, even_ref):
    size = own_ref.shape[1]
    for i, (own, pair) in enumerate(((own_ref, pair_ref), (core_ref, diag_ref))):
        odd, even = odd_even(own[...], pair[...])
        odd_ref[:, size * i : size * (i + 1)] = odd
        even_ref[:, size * i : size * (i + 1)] = even


def obs_kernel(obs_ref, precision_ref, counts_ref, keep_ref, send_ref):
    _, y, c = place()
    width = obs_ref.shape[2] // 2
    for day, ref in ((y, keep_ref), (1 - y, send_ref)):
        counts = counts_ref[day].astype(F32)
        for half, side in ((0, c), (1, 1 - c)):
            source = pl.ds(pl.multiple_of(side * width, width), width)
            target = pl.ds(half * width, width)
            ref[0, :, target] = obs_ref[day, :, source].astype(F32)
            ref[1, :, target] = counts * precision_ref[day, :, source].astype(F32)


def split(values):
    high = values.astype(BF16)
    return high, (values - high.astype(F32)).astype(BF16)


def banded(kern_ref, offset):
    forward = jnp.zeros(offset.shape, F32)
    adjoint = jnp.zeros(offset.shape, F32)
    for tap in range(TAPS):
        hit = offset == tap
        forward = jnp.where(hit, kern_ref[tap], forward)
        adjoint = jnp.where(hit, kern_ref[TAPS - 1 - tap], adjoint)
    return forward, adjoint


def matrix_kernel(pairs, rows, lat_ref, lon_ref, lat_fwd_ref, lat_adj_ref, lon_fwd_ref, lon_adj_ref):
    k, y, _ = place()
    dims = (2 * rows, 4 * rows)

    even = lax.rem(k, 2) == 0
    out = lax.broadcasted_iota(jnp.int32, dims, 0)
    col = lax.broadcasted_iota(jnp.int32, dims, 1)
    target = rows * jnp.where(y == 0, out // rows, 1 - out // rows) + out % rows
    source = rows * jnp.where(even, col // rows - 1, 2 - col // rows) + col % rows
    offset = source - target + HALF
    odd_open, even_open = open_sides(pairs)
    inside = jnp.where(col < 3 * rows, 1.0, even_open)
    inside = jnp.where(col < rows, odd_open, inside)
    for ref, matrix in zip((lat_fwd_ref, lat_adj_ref), banded(lat_ref, offset)):
        high, low = split(matrix * inside)
        ref[: 2 * rows, : 4 * rows] = high
        ref[: 2 * rows, 4 * rows :] = high
        ref[2 * rows :, : 4 * rows] = low
        ref[2 * rows :, 4 * rows :] = jnp.zeros(dims, BF16)
    dims = (EDGE, EDGE)
    offset = lax.broadcasted_iota(jnp.int32, dims, 0) - lax.broadcasted_iota(jnp.int32, dims, 1)
    for ref in (lon_fwd_ref, lon_adj_ref):
        ref[...] = jnp.zeros(ref.shape, BF16)
    for distance in range(3):
        pair = banded(lon_ref, offset + EDGE * distance - (EDGE - HALF))
        for ref, matrix in zip((lon_fwd_ref, lon_adj_ref), pair):
            for part, piece in enumerate(split(matrix)):
                for column in range(BLOCK // EDGE):
                    row = EDGE * (column + distance)
                    ref[part, row : row + EDGE, EDGE * column : EDGE * (column + 1)] = piece


def load(ref):
    if ref.shape[0] > 8:
        return ref[...]
    size, groups = ref.shape[1] // 2, HALF // 8
    width = (size - 128) // groups
    return jnp.concatenate(
        [
            jnp.concatenate(
                [ref[:, size * half + width * i : size * half + width * (i + 1)] for half in range(2)],
                axis=1,
            )
            for i in range(groups)
        ],
        axis=0,
    )


def edge_row(ref):
    size = ref.shape[1] // 2
    tiles = [ref[:, size * half - 128 : size * half] for half in (1, 2)]
    return jnp.concatenate([tile[i : i + 1, :] for tile in tiles for i in range(8)], axis=1)


def lat_conv(blocks, matrix_ref):
    high, low = split(jnp.concatenate(blocks, axis=0))
    stacked = jnp.concatenate([high, low], axis=0)
    both = jnp.dot(matrix_ref[...], stacked, preferred_element_type=F32)
    half = both.shape[0] // 2
    return both[:half] + both[half:]


def lon_conv(field, matrix_ref):
    rows, length = field.shape
    count = length // BLOCK
    parts = []
    for part in split(field):
        wide = jnp.concatenate([part[:, -EDGE:], part, part[:, :EDGE]], axis=1)
        parts += [wide[:, BLOCK * i : BLOCK * (i + 1) + 2 * EDGE] for i in range(count)]
    coarse = jnp.dot(jnp.concatenate(parts, axis=0), matrix_ref[0], preferred_element_type=F32)
    fine = jnp.dot(
        jnp.concatenate(parts[:count], axis=0), matrix_ref[1], preferred_element_type=F32
    )
    out = coarse[: count * rows] + coarse[count * rows :] + fine
    return jnp.concatenate([out[rows * i : rows * (i + 1)] for i in range(count)], axis=1)


def seen_kernel(*refs):
    lat_ref, fwd_ref, seen_ref = refs[4:]
    seen_ref[...] = lon_conv(lat_conv([load(ref) for ref in refs[:4]], lat_ref), fwd_ref)


def misfit_kernel(seen_ref, keep_ref, sent_ref, adj_ref, *outs):
    obs = jnp.concatenate([keep_ref[0], sent_ref[0]], axis=0)
    weight = jnp.concatenate([keep_ref[1], sent_ref[1]], axis=0)
    spread = lon_conv(weight * (obs - seen_ref[...]), adj_ref)
    rows, width = outs[0].shape
    odd, even = odd_even(spread[:rows], spread[rows:])
    for part, (odd_ref, even_ref) in enumerate(zip(outs[::2], outs[1::2])):
        columns = slice(width * part, width * (part + 1))
        odd_ref[...] = odd[:, columns]
        even_ref[...] = even[:, columns]


def beside(center, above, below):
    width = center.shape[1]
    lateral = pltpu.roll(center, 1, 1) + pltpu.roll(center, width - 1, 1)
    return above + below + lateral


def prior_kernel(pairs, *refs):
    fields = [load(ref) for ref in refs[:4]]
    odd_edge, even_edge = edge_row(refs[4]), edge_row(refs[5])
    out_ref, ext, wide, inner = refs[10:]
    k, y, _ = place()
    rows, length = fields[0].shape
    even = lax.rem(k, 2) == 0
    odd_open, even_open = open_sides(pairs)
    fields[0] = fields[0] * odd_open
    fields[3] = fields[3] * even_open
    for block, field in enumerate(fields):
        where = rows * jnp.where(even, block, 3 - block)
        ext[pl.ds(pl.multiple_of(where, rows), rows), :] = field
    for block, (left, right) in enumerate(map_pairs(refs[6:10])):
        where = pl.multiple_of(8 + rows * jnp.where(y == 0, block, 1 - block), 8)
        coef = jnp.concatenate([left[...], right[...]], axis=1) + 4.0
        wide[pl.ds(where, rows), :] = coef
    north = jnp.where(even, odd_edge, even_edge) + 4.0
    south = jnp.where(even, even_edge, odd_edge) + 4.0
    wide[:8, :] = jnp.broadcast_to(north, (8, length))
    wide[8 + 2 * rows :, :] = jnp.broadcast_to(south, (8, length))
    low, count = rows - 8, 2 * rows + 16
    center = ext[low : low + count, :]
    around = beside(center, ext[low - 1 : low - 1 + count, :], ext[low + 1 : low + 1 + count, :])
    inner[...] = wide[...] * center - around
    inner[:8, :] = inner[:8, :] * jnp.where(k == 0, 0.0, 1.0)
    inner[8 + 2 * rows :, :] = inner[8 + 2 * rows :, :] * jnp.where(k == pairs - 1, 0.0, 1.0)
    center = inner[8 : 8 + 2 * rows, :]
    around = beside(center, inner[7 : 7 + 2 * rows, :], inner[9 : 9 + 2 * rows, :])
    ext[: 2 * rows, :] = wide[8 : 8 + 2 * rows, :] * center - around
    out_ref[:rows, :] = ext[pl.ds(pl.multiple_of(rows * y, rows), rows), :]
    out_ref[rows:, :] = ext[pl.ds(pl.multiple_of(rows * (1 - y), rows), rows), :]


def map_pairs(refs):
    return refs[:2], refs[2:]


def adjoint_kernel(*refs):
    refs[5][...] = lat_conv([ref[...] for ref in refs[:4]], refs[4])


def update_kernel(back_ref, prior_ref, *refs):
    rows, width = back_ref.shape[0] // 2, back_ref.shape[1] // 2
    last = back_ref[...] - prior_ref[...]
    sea = [jnp.concatenate([left[...], right[...]], axis=1) for left, right in map_pairs(refs[:4])]
    last_own, last_pair = last[:rows] * sea[0], last[rows:] * sea[1]
    base, states, outs = refs[4:6], refs[6:8], refs[8:]
    for before, state, change in zip(base, states, odd_even(last_own, last_pair)):
        state[...] = load(before) + change * (1.0 / THETA)
    for i in range(2):
        outs[2 * i][...] = last_own[:, width * i : width * (i + 1)]
        outs[2 * i + 1][...] = last_pair[:, width * i : width * (i + 1)]


def last_kernel(half, *refs):
    lat_ref, prior_ref = refs[4:6]
    rows, width = refs[0].shape
    last = lat_conv([ref[...] for ref in refs[:4]], lat_ref)
    last = last - prior_ref[:, width * half : width * (half + 1)]
    own, pair = map_pairs(refs[6:10])
    refs[10][...] = last[:rows] * own[half][...]
    refs[11][...] = last[rows:] * pair[half][...]


def days_of():
    _, y, c = place()
    return 2 * c + y, 2 * c + (1 - y), 2 * (1 - c) + y, 2 * (1 - c) + (1 - y)


def early_kernel(*refs):
    guess_ref, land_ref, fixed_ref, state_ref = refs[4:]
    land = 1.0 - land_ref[...].astype(F32)
    for i, (day, ref) in enumerate(zip(days_of(), refs[:4])):
        guess = guess_ref[day]
        update = (ref[...] - land * guess) * (1.0 / THETA)
        state = guess + update
        fixed_ref[i] = land * state
        state_ref[i] = state + (NEW_RHO * RHO) * update


def final_kernel(half, *refs):
    late, (fixed_ref, sum_ref) = refs[:2], refs[2:4]
    state_ref, last_ref, state, last, sems = refs[-5:]
    days = days_of()[2 * half : 2 * half + 2]
    copies = []
    for i, (day, ref) in enumerate(zip(days, late)):
        last[i] = ref[...] - fixed_ref[2 * half + i]
        state[i] = sum_ref[2 * half + i] + (2.0 * NEW_RHO / DELTA) * last[i]
        for j, (source, target) in enumerate(((state, state_ref), (last, last_ref))):
            copies.append(pltpu.make_async_copy(source.at[i], target.at[day], sems.at[2 * i + j]))
            copies[-1].start()
    for copy in copies:
        copy.wait()


def body(
    pairs,
    first_guess,
    range_coef,
    land_sea,
    lat_kernel,
    lon_kernel,
    observations,
    obs_precision,
    track_counts,
):
    days, rows, width = first_guess.shape
    length = observations.shape[2]
    assert days == 4 and rows == HALF and length == 2 * width and length % BLOCK == 0
    assert width == 8 * 128
    places = [(k, y, c) for k in range(pairs) for y in range(2) for c in range(2)]

    def permute(array, move):
        moves = [(i, places.index(move(*at))) for i, at in enumerate(places)]
        return lax.ppermute(array, AXES, moves)

    def swap(k, y, c, parity):
        target = k + 1 if k % 2 == parity else k - 1
        return (target, y, c) if 0 <= target < pairs else (k, y, 1 - c)

    core = lambda array: permute(array, lambda k, y, c: (k, y, 1 - c))
    pair = lambda array: permute(array, lambda k, y, c: (k, 1 - y, c))
    diag = lambda array: permute(array, lambda k, y, c: (k, 1 - y, 1 - c))
    odd = lambda array: permute(array, lambda k, y, c: swap(k, y, c, 1))
    even = lambda array: permute(array, lambda k, y, c: swap(k, y, c, 0))

    piece = shape(rows, width)
    packed = shape(8, rows // 8 * width + 128)
    own, to_core, to_pair, to_diag = call(
        pack_kernel,
        [packed] * 4,
        [first_guess, land_sea, range_coef],
        [HBM] * 3,
        scratch=[
            pltpu.VMEM((4, rows, width), F32),
            pltpu.VMEM((rows, width), jnp.int32),
            pltpu.VMEM((8, width), F32),
            pltpu.VMEM((4,) + packed.shape, F32),
            pltpu.SemaphoreType.DMA((10,)),
        ],
        outs=[HBM] * 4,
        vmem=PACK_VMEM,
        name="pack",
    )
    by_pair, by_diag = pair(to_pair), diag(to_diag)
    observations, own = lax.optimization_barrier((observations, own))
    by_core = core(to_core)
    keep, send = call(
        obs_kernel,
        [shape(2, rows, length)] * 2,
        [observations, obs_precision, track_counts[:, :, None]],
        name="observed",
    )
    coef, sea = range_coef, land_sea.astype(F32)
    send, by_pair, by_diag, by_core = lax.optimization_barrier((send, by_pair, by_diag, by_core))
    sent = pair(send)
    v_odd, v_even = call(
        order_kernel,
        [shape(8, 2 * packed.shape[1])] * 2,
        [own, by_core, by_pair, by_diag],
        name="order",
    )
    coef, sea, lat_kernel, v_odd = lax.optimization_barrier((coef, sea, lat_kernel, v_odd))
    lat_fwd, lat_adj, lon_fwd, lon_adj = call(
        functools.partial(matrix_kernel, pairs, rows),
        [shape(4 * rows, 8 * rows, dtype=BF16)] * 2
        + [shape(2, BLOCK + 2 * EDGE, BLOCK, dtype=BF16)] * 2,
        [lat_kernel, lon_kernel],
        [SMEM, SMEM],
        flops=4 * 65 * 2 * 70000,
        name="matrices",
    )
    fields = [odd(v_odd), v_odd, v_even, even(v_even)]
    by_lon = [core(coef), core(sea)]
    fields[0], *by_lon = lax.optimization_barrier((fields[0], *by_lon))
    edges = [fields[0], fields[3]]
    band = shape(rows, length)
    conv = 2 * 3 * 2 * rows * length * 512
    for step in range(2):
        (seen,) = call(
            seen_kernel,
            [shape(2 * rows, length)],
            fields + [lat_fwd, lon_fwd],
            flops=2 * conv,
            name="seen",
        )
        misfit = call(
            misfit_kernel,
            [piece] * 4 if step else [band] * 2,
            [seen, keep, sent, lon_adj],
            flops=conv,
            name="misfit",
        )
        if not step:
            coef, sea, misfit[0] = lax.optimization_barrier((coef, sea, misfit[0]))
            coef_pair, sea_pair = pair(coef), pair(sea)
            coefs = [coef, by_lon[0], coef_pair, core(coef_pair)]
            seas = [sea, by_lon[1], sea_pair, core(sea_pair)]
        (prior,) = call(
            functools.partial(prior_kernel, pairs),
            [shape(2 * rows, length)],
            fields + edges + coefs,
            scratch=[
                pltpu.VMEM((4 * rows, length), F32),
                pltpu.VMEM((2 * rows + 16, length), F32),
                pltpu.VMEM((2 * rows + 16, length), F32),
            ],
            name="prior",
        )
        common = [lat_adj, prior] + seas
        moved = [odd(m) if i % 2 == 0 else even(m) for i, m in enumerate(misfit)]
        if not step:
            (back,) = call(
                adjoint_kernel,
                [shape(2 * rows, length)],
                [moved[0], *misfit, moved[1], lat_adj],
                flops=ADJOINT_COST,
                name="adjoint",
            )
            v_odd, v_even, *pieces = call(
                update_kernel,
                [band] * 2 + [piece] * 4,
                [back, prior, *seas, v_odd, v_even],
                name="update",
            )
            fields = [odd(v_odd), v_odd, v_even, even(v_even)]
            pieces = [pieces[0], pair(pieces[1]), core(pieces[2]), diag(pieces[3])]
            early = call(
                early_kernel,
                [shape(days, rows, width)] * 2,
                pieces + [first_guess, land_sea],
                name="early",
            )
    moved[0], *early = lax.optimization_barrier((moved[0], *early))
    left_own, left_pair = call(
        functools.partial(last_kernel, 0),
        [piece] * 2,
        [moved[0], *misfit[:2], moved[1], *common],
        flops=LEFT_COST,
        name="update",
    )
    moved[2], left_own = lax.optimization_barrier((moved[2], left_own))
    right_own, right_pair = call(
        functools.partial(last_kernel, 1),
        [piece] * 2,
        [moved[2], *misfit[2:], moved[3], *common],
        flops=conv,
        name="update",
    )
    pieces = [left_own, pair(left_pair), core(right_own), diag(right_pair)]
    result = []
    for half in range(2):
        args = pieces[2 * half : 2 * half + 2] + early
        result = call(
            functools.partial(final_kernel, half),
            [shape(days, rows, width)] * 2,
            args + (result if half else []),
            [VMEM] * 4 + [HBM] * 2 * half,
            outs=[HBM] * 2,
            scratch=[
                pltpu.VMEM((2, rows, width), F32),
                pltpu.VMEM((2, rows, width), F32),
                pltpu.SemaphoreType.DMA((4,)),
            ],
            aliases={4: 0, 5: 1} if half else {},
            flops=0 if half else LEFT_COST,
            name="final",
        )
    return tuple(result)


def solution(mesh):
    assert mesh.shape["lat"] % 2 == 0 and mesh.shape["lon"] == 2
    in_specs = (
        P(None, ("groups", "lat"), "lon"),
        P(("groups", "lat"), "lon"),
        P(("groups", "lat"), "lon"),
        P(),
        P(),
        P("lon", ("groups", "lat"), None),
        P("lon", ("groups", "lat"), None),
        P("lon", ("groups", "lat")),
    )
    out_specs = (P(None, ("groups", "lat"), "lon"), P(None, ("groups", "lat"), "lon"))
    return jax.shard_map(
        functools.partial(body, mesh.shape["lat"] // 2),
        mesh=mesh,
        in_specs=in_specs,
        out_specs=out_specs,
        check_vma=False,
    )
```

```python
import functools

import jax
import jax.numpy as jnp
from jax import lax
from jax.experimental import pallas as pl
from jax.experimental.pallas import tpu as pltpu
from jax.sharding import PartitionSpec as P

HALF = 32
TAPS = 2 * HALF + 1
LOWER = 0.25
UPPER = 120.0
THETA = (LOWER + UPPER) / 2.0
DELTA = (UPPER - LOWER) / 2.0
SIGMA = THETA / DELTA
RHO = 1.0 / SIGMA
NEW_RHO = 1.0 / (2.0 * SIGMA - RHO)
BLOCK = 256
EDGE = 128
LEFT_COST = 5 * 10**9
ADJOINT_COST = 2 * 10**10
PACK_VMEM = 62 * 2**20
AXES = ("lat", "lon")

VMEM = pl.BlockSpec(memory_space=pltpu.VMEM)
SMEM = pl.BlockSpec(memory_space=pltpu.SMEM)
HBM = pl.BlockSpec(memory_space=pltpu.HBM)
F32 = jnp.float32
BF16 = jnp.bfloat16


def place():
    lat = lax.axis_index("lat")
    return lat // 2, lax.rem(lat, 2), lax.axis_index("lon")


def open_sides(pairs):
    k, _, _ = place()
    north, south = jnp.where(k == 0, 0.0, 1.0), jnp.where(k == pairs - 1, 0.0, 1.0)
    flip = lax.rem(k, 2) == 1
    return jnp.where(flip, north, south), jnp.where(flip, south, north)


def lead_trail(own, pair):
    k, y, _ = place()
    straight = lax.rem(k + y, 2) == 1
    return jnp.where(straight, own, pair), jnp.where(straight, pair, own)


def shape(*dims, dtype=F32):
    return jax.ShapeDtypeStruct(dims, dtype)


def call(
    kernel, out_shape, args, specs=None, outs=None, scratch=(), flops=0, vmem=24 * 2**20, aliases=None, name=None
):
    nbytes = 0 if flops == 0 else sum(a.size * a.dtype.itemsize for a in args)
    return list(pl.pallas_call(
        kernel,
        out_shape=out_shape,
        in_specs=specs or [VMEM] * len(args),
        out_specs=outs or [VMEM] * len(out_shape),
        scratch_shapes=list(scratch),
        input_output_aliases=aliases or {},
        compiler_params=pltpu.CompilerParams(vmem_limit_bytes=vmem),
        cost_estimate=pl.CostEstimate(flops=flops, bytes_accessed=nbytes, transcendentals=0),
        name=name,
    )(*args))


def pack_kernel(guess_ref, land_ref, coef_ref, own_ref, core_ref, pair_ref, diag_ref, *scratch):
    guess, land, coef, packed, sems = scratch
    _, y, c = place()
    days = (2 * c + (1 - y), 2 * (1 - c) + (1 - y), 2 * (1 - c) + y, 2 * c + y)
    rows, width = land.shape
    start = pl.multiple_of((rows - 8) * y, 8)
    copies = [
        pltpu.make_async_copy(land_ref, land, sems.at[0]),
        pltpu.make_async_copy(coef_ref.at[pl.ds(start, 8), :], coef, sems.at[1]),
    ]
    for i, day in enumerate(days):
        copies.append(pltpu.make_async_copy(guess_ref.at[day], guess.at[i], sems.at[2 + i]))
    for copy in copies:
        copy.start()
    copies[0].wait()
    copies[1].wait()
    edge = jnp.where(y == 0, coef[:1, :], coef[7:, :])
    edge = jnp.concatenate([edge[:, i : i + 128] for i in range(0, width, 128)], axis=0)
    outs = []
    for i, ref in enumerate((pair_ref, diag_ref, core_ref, own_ref)):
        copies[2 + i].wait()
        for group in range(rows // 8):
            part = slice(8 * group, 8 * group + 8)
            sea = land[part, :].astype(F32)
            packed[i, :, width * group : width * (group + 1)] = guess[i, part, :] * sea
        packed[i, :, width * (rows // 8) :] = edge
        outs.append(pltpu.make_async_copy(packed.at[i], ref, sems.at[6 + i]))
        outs[-1].start()
    for out in outs:
        out.wait()


def order_kernel(own_ref, core_ref, pair_ref, diag_ref, lead_ref, trail_ref):
    size = own_ref.shape[1]
    for i, (own, pair) in enumerate(((own_ref, pair_ref), (core_ref, diag_ref))):
        lead, trail = lead_trail(own[...], pair[...])
        lead_ref[:, size * i : size * (i + 1)] = lead
        trail_ref[:, size * i : size * (i + 1)] = trail


def obs_kernel(obs_ref, precision_ref, counts_ref, keep_ref, send_ref):
    _, y, c = place()
    width = obs_ref.shape[2] // 2
    for day, ref in ((y, keep_ref), (1 - y, send_ref)):
        counts = counts_ref[day].astype(F32)
        for half, side in ((0, c), (1, 1 - c)):
            source = pl.ds(pl.multiple_of(side * width, width), width)
            target = pl.ds(half * width, width)
            ref[0, :, target] = obs_ref[day, :, source].astype(F32)
            ref[1, :, target] = counts * precision_ref[day, :, source].astype(F32)


def split(values):
    high = values.astype(BF16)
    return high, (values - high.astype(F32)).astype(BF16)


def banded(kern_ref, offset):
    forward = jnp.zeros(offset.shape, F32)
    adjoint = jnp.zeros(offset.shape, F32)
    for tap in range(TAPS):
        hit = offset == tap
        forward = jnp.where(hit, kern_ref[tap], forward)
        adjoint = jnp.where(hit, kern_ref[TAPS - 1 - tap], adjoint)
    return forward, adjoint


def matrix_kernel(pairs, rows, lat_ref, lon_ref, lat_fwd_ref, lat_adj_ref, lon_fwd_ref, lon_adj_ref):
    k, y, _ = place()
    dims = (2 * rows, 4 * rows)

    flip = lax.rem(k, 2) == 1
    out = lax.broadcasted_iota(jnp.int32, dims, 0)
    col = lax.broadcasted_iota(jnp.int32, dims, 1)
    target = rows * jnp.where(y == 0, out // rows, 1 - out // rows) + out % rows
    source = rows * jnp.where(flip, col // rows - 1, 2 - col // rows) + col % rows
    offset = source - target + HALF
    lead_open, trail_open = open_sides(pairs)
    inside = jnp.where(col < 3 * rows, 1.0, trail_open)
    inside = jnp.where(col < rows, lead_open, inside)
    for ref, matrix in zip((lat_fwd_ref, lat_adj_ref), banded(lat_ref, offset)):
        high, low = split(matrix * inside)
        ref[: 2 * rows, : 4 * rows] = high
        ref[: 2 * rows, 4 * rows :] = high
        ref[2 * rows :, : 4 * rows] = low
        ref[2 * rows :, 4 * rows :] = jnp.zeros(dims, BF16)
    dims = (EDGE, EDGE)
    offset = lax.broadcasted_iota(jnp.int32, dims, 0) - lax.broadcasted_iota(jnp.int32, dims, 1)
    for ref in (lon_fwd_ref, lon_adj_ref):
        ref[...] = jnp.zeros(ref.shape, BF16)
    for distance in range(3):
        pair = banded(lon_ref, offset + EDGE * distance - (EDGE - HALF))
        for ref, matrix in zip((lon_fwd_ref, lon_adj_ref), pair):
            for part, piece in enumerate(split(matrix)):
                for column in range(BLOCK // EDGE):
                    row = EDGE * (column + distance)
                    ref[part, row : row + EDGE, EDGE * column : EDGE * (column + 1)] = piece


def load(ref):
    if ref.shape[0] > 8:
        return ref[...]
    size, groups = ref.shape[1] // 2, HALF // 8
    width = (size - 128) // groups
    return jnp.concatenate(
        [
            jnp.concatenate(
                [ref[:, size * half + width * i : size * half + width * (i + 1)] for half in range(2)],
                axis=1,
            )
            for i in range(groups)
        ],
        axis=0,
    )


def edge_row(ref):
    size = ref.shape[1] // 2
    tiles = [ref[:, size * half - 128 : size * half] for half in (1, 2)]
    return jnp.concatenate([tile[i : i + 1, :] for tile in tiles for i in range(8)], axis=1)


def lat_conv(blocks, matrix_ref):
    high, low = split(jnp.concatenate(blocks, axis=0))
    stacked = jnp.concatenate([high, low], axis=0)
    both = jnp.dot(matrix_ref[...], stacked, preferred_element_type=F32)
    half = both.shape[0] // 2
    return both[:half] + both[half:]


def lon_conv(field, matrix_ref):
    rows, length = field.shape
    count = length // BLOCK
    parts = []
    for part in split(field):
        wide = jnp.concatenate([part[:, -EDGE:], part, part[:, :EDGE]], axis=1)
        parts += [wide[:, BLOCK * i : BLOCK * (i + 1) + 2 * EDGE] for i in range(count)]
    coarse = jnp.dot(jnp.concatenate(parts, axis=0), matrix_ref[0], preferred_element_type=F32)
    fine = jnp.dot(
        jnp.concatenate(parts[:count], axis=0), matrix_ref[1], preferred_element_type=F32
    )
    out = coarse[: count * rows] + coarse[count * rows :] + fine
    return jnp.concatenate([out[rows * i : rows * (i + 1)] for i in range(count)], axis=1)


def seen_kernel(*refs):
    lat_ref, fwd_ref, seen_ref = refs[4:]
    seen_ref[...] = lon_conv(lat_conv([load(ref) for ref in refs[:4]], lat_ref), fwd_ref)


def misfit_kernel(seen_ref, keep_ref, sent_ref, adj_ref, *outs):
    obs = jnp.concatenate([keep_ref[0], sent_ref[0]], axis=0)
    weight = jnp.concatenate([keep_ref[1], sent_ref[1]], axis=0)
    spread = lon_conv(weight * (obs - seen_ref[...]), adj_ref)
    rows, width = outs[0].shape
    lead, trail = lead_trail(spread[:rows], spread[rows:])
    for part, (lead_ref, trail_ref) in enumerate(zip(outs[::2], outs[1::2])):
        columns = slice(width * part, width * (part + 1))
        lead_ref[...] = lead[:, columns]
        trail_ref[...] = trail[:, columns]


def beside(center, above, below):
    width = center.shape[1]
    lateral = pltpu.roll(center, 1, 1) + pltpu.roll(center, width - 1, 1)
    return above + below + lateral


def prior_kernel(pairs, *refs):
    fields = [load(ref) for ref in refs[:4]]
    lead_edge, trail_edge = edge_row(refs[4]), edge_row(refs[5])
    out_ref, ext, wide, inner = refs[10:]
    k, y, _ = place()
    rows, length = fields[0].shape
    flip = lax.rem(k, 2) == 1
    lead_open, trail_open = open_sides(pairs)
    fields[0] = fields[0] * lead_open
    fields[3] = fields[3] * trail_open
    for block, field in enumerate(fields):
        where = rows * jnp.where(flip, block, 3 - block)
        ext[pl.ds(pl.multiple_of(where, rows), rows), :] = field
    for block, (left, right) in enumerate(map_pairs(refs[6:10])):
        where = pl.multiple_of(8 + rows * jnp.where(y == 0, block, 1 - block), 8)
        coef = jnp.concatenate([left[0], right[0]], axis=1) + 4.0
        wide[pl.ds(where, rows), :] = coef
    north = jnp.where(flip, lead_edge, trail_edge) + 4.0
    south = jnp.where(flip, trail_edge, lead_edge) + 4.0
    wide[:8, :] = jnp.broadcast_to(north, (8, length))
    wide[8 + 2 * rows :, :] = jnp.broadcast_to(south, (8, length))
    low, count = rows - 8, 2 * rows + 16
    center = ext[low : low + count, :]
    around = beside(center, ext[low - 1 : low - 1 + count, :], ext[low + 1 : low + 1 + count, :])
    inner[...] = wide[...] * center - around
    inner[:8, :] = inner[:8, :] * jnp.where(k == 0, 0.0, 1.0)
    inner[8 + 2 * rows :, :] = inner[8 + 2 * rows :, :] * jnp.where(k == pairs - 1, 0.0, 1.0)
    center = inner[8 : 8 + 2 * rows, :]
    around = beside(center, inner[7 : 7 + 2 * rows, :], inner[9 : 9 + 2 * rows, :])
    ext[: 2 * rows, :] = wide[8 : 8 + 2 * rows, :] * center - around
    out_ref[:rows, :] = ext[pl.ds(pl.multiple_of(rows * y, rows), rows), :]
    out_ref[rows:, :] = ext[pl.ds(pl.multiple_of(rows * (1 - y), rows), rows), :]


def map_pairs(refs):
    return refs[:2], refs[2:]


def adjoint_kernel(*refs):
    refs[5][...] = lat_conv([ref[...] for ref in refs[:4]], refs[4])


def update_kernel(back_ref, prior_ref, *refs):
    rows, width = back_ref.shape[0] // 2, back_ref.shape[1] // 2
    last = back_ref[...] - prior_ref[...]
    sea = [jnp.concatenate([left[1], right[1]], axis=1) for left, right in map_pairs(refs[:4])]
    last_own, last_pair = last[:rows] * sea[0], last[rows:] * sea[1]
    base, states, outs = refs[4:6], refs[6:8], refs[8:]
    for before, state, change in zip(base, states, lead_trail(last_own, last_pair)):
        state[...] = load(before) + change * (1.0 / THETA)
    for i in range(2):
        outs[2 * i][...] = last_own[:, width * i : width * (i + 1)]
        outs[2 * i + 1][...] = last_pair[:, width * i : width * (i + 1)]


def last_kernel(half, *refs):
    lat_ref, prior_ref = refs[4:6]
    rows, width = refs[0].shape
    last = lat_conv([ref[...] for ref in refs[:4]], lat_ref)
    last = last - prior_ref[:, width * half : width * (half + 1)]
    own, pair = map_pairs(refs[6:10])
    refs[10][...] = last[:rows] * own[half][1]
    refs[11][...] = last[rows:] * pair[half][1]


def days_of():
    _, y, c = place()
    return 2 * c + y, 2 * c + (1 - y), 2 * (1 - c) + y, 2 * (1 - c) + (1 - y)


def early_kernel(*refs):
    guess_ref, land_ref, fixed_ref, state_ref = refs[4:]
    land = 1.0 - land_ref[...].astype(F32)
    for i, (day, ref) in enumerate(zip(days_of(), refs[:4])):
        guess = guess_ref[day]
        update = (ref[...] - land * guess) * (1.0 / THETA)
        state = guess + update
        fixed_ref[i] = land * state
        state_ref[i] = state + (NEW_RHO * RHO) * update


def final_kernel(half, *refs):
    late, (fixed_ref, sum_ref) = refs[:2], refs[2:4]
    state_ref, last_ref, state, last, sems = refs[-5:]
    days = days_of()[2 * half : 2 * half + 2]
    copies = []
    for i, (day, ref) in enumerate(zip(days, late)):
        last[i] = ref[...] - fixed_ref[2 * half + i]
        state[i] = sum_ref[2 * half + i] + (2.0 * NEW_RHO / DELTA) * last[i]
        for j, (source, target) in enumerate(((state, state_ref), (last, last_ref))):
            copies.append(pltpu.make_async_copy(source.at[i], target.at[day], sems.at[2 * i + j]))
            copies[-1].start()
    for copy in copies:
        copy.wait()


def body(
    pairs,
    first_guess,
    range_coef,
    land_sea,
    lat_kernel,
    lon_kernel,
    observations,
    obs_precision,
    track_counts,
):
    days, rows, width = first_guess.shape
    length = observations.shape[2]
    assert days == 4 and rows == HALF and length == 2 * width and length % BLOCK == 0
    assert width == 8 * 128
    places = [(k, y, c) for k in range(pairs) for y in range(2) for c in range(2)]

    def permute(array, move):
        moves = [(i, places.index(move(*at))) for i, at in enumerate(places)]
        return lax.ppermute(array, AXES, moves)

    def swap(k, y, c, parity):
        target = k + 1 if k % 2 == parity else k - 1
        return (target, y, c) if 0 <= target < pairs else (k, y, 1 - c)

    core = lambda array: permute(array, lambda k, y, c: (k, y, 1 - c))
    pair = lambda array: permute(array, lambda k, y, c: (k, 1 - y, c))
    diag = lambda array: permute(array, lambda k, y, c: (k, 1 - y, 1 - c))
    lead = lambda array: permute(array, lambda k, y, c: swap(k, y, c, 0))
    trail = lambda array: permute(array, lambda k, y, c: swap(k, y, c, 1))

    piece = shape(rows, width)
    packed = shape(8, rows // 8 * width + 128)
    own, to_core, to_pair, to_diag = call(
        pack_kernel,
        [packed] * 4,
        [first_guess, land_sea, range_coef],
        [HBM] * 3,
        scratch=[
            pltpu.VMEM((4, rows, width), F32),
            pltpu.VMEM((rows, width), jnp.int32),
            pltpu.VMEM((8, width), F32),
            pltpu.VMEM((4,) + packed.shape, F32),
            pltpu.SemaphoreType.DMA((10,)),
        ],
        outs=[HBM] * 4,
        vmem=PACK_VMEM,
        name="pack",
    )
    by_pair, by_diag = pair(to_pair), diag(to_diag)
    observations, own = lax.optimization_barrier((observations, own))
    by_core = core(to_core)
    keep, send = call(
        obs_kernel,
        [shape(2, rows, length)] * 2,
        [observations, obs_precision, track_counts[:, :, None]],
        name="observed",
    )
    maps = jnp.stack([range_coef, land_sea.astype(F32)])
    sent = pair(send)
    v_lead, v_trail = call(
        order_kernel,
        [shape(8, 2 * packed.shape[1])] * 2,
        [own, by_core, by_pair, by_diag],
        flops=ADJOINT_COST,
        name="order",
    )
    maps, lat_kernel, v_lead = lax.optimization_barrier((maps, lat_kernel, v_lead))
    lat_fwd, lat_adj, lon_fwd, lon_adj = call(
        functools.partial(matrix_kernel, pairs, rows),
        [shape(4 * rows, 8 * rows, dtype=BF16)] * 2
        + [shape(2, BLOCK + 2 * EDGE, BLOCK, dtype=BF16)] * 2,
        [lat_kernel, lon_kernel],
        [SMEM, SMEM],
        flops=4 * 65 * 2 * 70000,
        name="matrices",
    )
    fields = [lead(v_lead), v_lead, v_trail, trail(v_trail)]
    by_lon = core(maps)
    fields[0], by_lon = lax.optimization_barrier((fields[0], by_lon))
    edges = [fields[0], fields[3]]
    band = shape(rows, length)
    conv = 2 * 3 * 2 * rows * length * 512
    for step in range(2):
        (seen,) = call(
            seen_kernel,
            [shape(2 * rows, length)],
            fields + [lat_fwd, lon_fwd],
            flops=2 * conv,
            name="seen",
        )
        misfit = call(
            misfit_kernel,
            [piece] * 4 if step else [band] * 2,
            [seen, keep, sent, lon_adj],
            flops=conv,
            name="misfit",
        )
        if not step:
            maps, misfit[0] = lax.optimization_barrier((maps, misfit[0]))
            maps_pair = pair(maps)
            maps = [maps, by_lon, maps_pair, core(maps_pair)]
        (prior,) = call(
            functools.partial(prior_kernel, pairs),
            [shape(2 * rows, length)],
            fields + edges + maps,
            scratch=[
                pltpu.VMEM((4 * rows, length), F32),
                pltpu.VMEM((2 * rows + 16, length), F32),
                pltpu.VMEM((2 * rows + 16, length), F32),
            ],
            name="prior",
        )
        common = [lat_adj, prior] + maps
        moved = [lead(m) if i % 2 == 0 else trail(m) for i, m in enumerate(misfit)]
        if not step:
            (back,) = call(
                adjoint_kernel,
                [shape(2 * rows, length)],
                [moved[0], *misfit, moved[1], lat_adj],
                flops=ADJOINT_COST,
                name="adjoint",
            )
            v_lead, v_trail, *pieces = call(
                update_kernel,
                [band] * 2 + [piece] * 4,
                [back, prior, *maps, v_lead, v_trail],
                name="update",
            )
            fields = [lead(v_lead), v_lead, v_trail, trail(v_trail)]
            pieces = [pieces[0], pair(pieces[1]), core(pieces[2]), diag(pieces[3])]
            early = call(
                early_kernel,
                [shape(days, rows, width)] * 2,
                pieces + [first_guess, land_sea],
                name="early",
            )
    moved[0], *early = lax.optimization_barrier((moved[0], *early))
    left_own, left_pair = call(
        functools.partial(last_kernel, 0),
        [piece] * 2,
        [moved[0], *misfit[:2], moved[1], *common],
        flops=LEFT_COST,
        name="update",
    )
    moved[2], left_own = lax.optimization_barrier((moved[2], left_own))
    right_own, right_pair = call(
        functools.partial(last_kernel, 1),
        [piece] * 2,
        [moved[2], *misfit[2:], moved[3], *common],
        flops=conv,
        name="update",
    )
    pieces = [left_own, pair(left_pair), core(right_own), diag(right_pair)]
    result = []
    for half in range(2):
        args = pieces[2 * half : 2 * half + 2] + early
        result = call(
            functools.partial(final_kernel, half),
            [shape(days, rows, width)] * 2,
            args + (result if half else []),
            [VMEM] * 4 + [HBM] * 2 * half,
            outs=[HBM] * 2,
            scratch=[
                pltpu.VMEM((2, rows, width), F32),
                pltpu.VMEM((2, rows, width), F32),
                pltpu.SemaphoreType.DMA((4,)),
            ],
            aliases={4: 0, 5: 1} if half else {},
            flops=0 if half else LEFT_COST,
            name="final",
        )
    return tuple(result)


def solution(mesh):
    assert mesh.shape["lat"] % 2 == 0 and mesh.shape["lon"] == 2
    in_specs = (
        P(None, ("groups", "lat"), "lon"),
        P(("groups", "lat"), "lon"),
        P(("groups", "lat"), "lon"),
        P(),
        P(),
        P("lon", ("groups", "lat"), None),
        P("lon", ("groups", "lat"), None),
        P("lon", ("groups", "lat")),
    )
    out_specs = (P(None, ("groups", "lat"), "lon"), P(None, ("groups", "lat"), "lon"))
    return jax.shard_map(
        functools.partial(body, mesh.shape["lat"] // 2),
        mesh=mesh,
        in_specs=in_specs,
        out_specs=out_specs,
        check_vma=False,
    )
```

```python
import functools

import jax
import jax.numpy as jnp
from jax import lax
from jax.experimental import pallas as pl
from jax.experimental.pallas import tpu as pltpu
from jax.sharding import PartitionSpec as P

HALF = 32
TAPS = 2 * HALF + 1
LOWER = 0.25
UPPER = 120.0
THETA = (LOWER + UPPER) / 2.0
DELTA = (UPPER - LOWER) / 2.0
SIGMA = THETA / DELTA
RHO = 1.0 / SIGMA
NEW_RHO = 1.0 / (2.0 * SIGMA - RHO)
BLOCK = 256
EDGE = 128
LEFT_COST = 5 * 10**9
ADJOINT_COST = 2 * 10**10
PACK_VMEM = 62 * 2**20
AXES = ("lat", "lon")

VMEM = pl.BlockSpec(memory_space=pltpu.VMEM)
SMEM = pl.BlockSpec(memory_space=pltpu.SMEM)
HBM = pl.BlockSpec(memory_space=pltpu.HBM)
F32 = jnp.float32
BF16 = jnp.bfloat16


def place():
    lat = lax.axis_index("lat")
    return lat // 2, lax.rem(lat, 2), lax.axis_index("lon")


def open_sides(pairs):
    k, _, _ = place()
    north, south = jnp.where(k == 0, 0.0, 1.0), jnp.where(k == pairs - 1, 0.0, 1.0)
    flip = lax.rem(k, 2) == 1
    return jnp.where(flip, north, south), jnp.where(flip, south, north)


def lead_trail(own, pair):
    k, y, _ = place()
    straight = lax.rem(k + y, 2) == 1
    return jnp.where(straight, own, pair), jnp.where(straight, pair, own)


def shape(*dims, dtype=F32):
    return jax.ShapeDtypeStruct(dims, dtype)


def call(
    kernel, out_shape, args, specs=None, outs=None, scratch=(), flops=0, vmem=24 * 2**20, aliases=None, name=None
):
    nbytes = 0 if flops == 0 else sum(a.size * a.dtype.itemsize for a in args)
    return list(pl.pallas_call(
        kernel,
        out_shape=out_shape,
        in_specs=specs or [VMEM] * len(args),
        out_specs=outs or [VMEM] * len(out_shape),
        scratch_shapes=list(scratch),
        input_output_aliases=aliases or {},
        compiler_params=pltpu.CompilerParams(vmem_limit_bytes=vmem),
        cost_estimate=pl.CostEstimate(flops=flops, bytes_accessed=nbytes, transcendentals=0),
        name=name,
    )(*args))


def pack_kernel(guess_ref, land_ref, coef_ref, own_ref, core_ref, pair_ref, diag_ref, *scratch):
    guess, land, coef, packed, sems = scratch
    _, y, c = place()
    days = (2 * c + (1 - y), 2 * (1 - c) + (1 - y), 2 * (1 - c) + y, 2 * c + y)
    rows, width = land.shape
    start = pl.multiple_of((rows - 8) * y, 8)
    copies = [
        pltpu.make_async_copy(land_ref, land, sems.at[0]),
        pltpu.make_async_copy(coef_ref.at[pl.ds(start, 8), :], coef, sems.at[1]),
    ]
    for i, day in enumerate(days):
        copies.append(pltpu.make_async_copy(guess_ref.at[day], guess.at[i], sems.at[2 + i]))
    for copy in copies:
        copy.start()
    copies[0].wait()
    copies[1].wait()
    edge = jnp.where(y == 0, coef[:1, :], coef[7:, :])
    edge = jnp.concatenate([edge[:, i : i + 128] for i in range(0, width, 128)], axis=0)
    outs = []
    for i, ref in enumerate((pair_ref, diag_ref, core_ref, own_ref)):
        copies[2 + i].wait()
        for group in range(rows // 8):
            part = slice(8 * group, 8 * group + 8)
            sea = land[part, :].astype(F32)
            packed[i, :, width * group : width * (group + 1)] = guess[i, part, :] * sea
        packed[i, :, width * (rows // 8) :] = edge
        outs.append(pltpu.make_async_copy(packed.at[i], ref, sems.at[6 + i]))
        outs[-1].start()
    for out in outs:
        out.wait()


def order_kernel(own_ref, pair_ref, diag_ref, core_ref, lead_ref, trail_ref):
    size = own_ref.shape[1]
    for i, (own, pair) in enumerate(((own_ref, pair_ref), (core_ref, diag_ref))):
        lead, trail = lead_trail(own[...], pair[...])
        lead_ref[:, size * i : size * (i + 1)] = lead
        trail_ref[:, size * i : size * (i + 1)] = trail


def obs_kernel(obs_ref, precision_ref, counts_ref, keep_ref, send_ref):
    _, y, c = place()
    width = obs_ref.shape[2] // 2
    for day, ref in ((y, keep_ref), (1 - y, send_ref)):
        counts = counts_ref[day].astype(F32)
        for half, side in ((0, c), (1, 1 - c)):
            source = pl.ds(pl.multiple_of(side * width, width), width)
            target = pl.ds(half * width, width)
            ref[0, :, target] = obs_ref[day, :, source].astype(F32)
            ref[1, :, target] = counts * precision_ref[day, :, source].astype(F32)


def split(values):
    high = values.astype(BF16)
    return high, (values - high.astype(F32)).astype(BF16)


def banded(kern_ref, offset):
    forward = jnp.zeros(offset.shape, F32)
    adjoint = jnp.zeros(offset.shape, F32)
    for tap in range(TAPS):
        hit = offset == tap
        forward = jnp.where(hit, kern_ref[tap], forward)
        adjoint = jnp.where(hit, kern_ref[TAPS - 1 - tap], adjoint)
    return forward, adjoint


def matrix_kernel(pairs, rows, lat_ref, lon_ref, lat_fwd_ref, lat_adj_ref, lon_fwd_ref, lon_adj_ref):
    k, y, _ = place()
    dims = (2 * rows, 4 * rows)

    flip = lax.rem(k, 2) == 1
    out = lax.broadcasted_iota(jnp.int32, dims, 0)
    col = lax.broadcasted_iota(jnp.int32, dims, 1)
    target = rows * jnp.where(y == 0, out // rows, 1 - out // rows) + out % rows
    source = rows * jnp.where(flip, col // rows - 1, 2 - col // rows) + col % rows
    offset = source - target + HALF
    lead_open, trail_open = open_sides(pairs)
    inside = jnp.where(col < 3 * rows, 1.0, trail_open)
    inside = jnp.where(col < rows, lead_open, inside)
    for ref, matrix in zip((lat_fwd_ref, lat_adj_ref), banded(lat_ref, offset)):
        high, low = split(matrix * inside)
        ref[: 2 * rows, : 4 * rows] = high
        ref[: 2 * rows, 4 * rows :] = high
        ref[2 * rows :, : 4 * rows] = low
        ref[2 * rows :, 4 * rows :] = jnp.zeros(dims, BF16)
    dims = (EDGE, EDGE)
    offset = lax.broadcasted_iota(jnp.int32, dims, 0) - lax.broadcasted_iota(jnp.int32, dims, 1)
    for ref in (lon_fwd_ref, lon_adj_ref):
        ref[...] = jnp.zeros(ref.shape, BF16)
    for distance in range(3):
        pair = banded(lon_ref, offset + EDGE * distance - (EDGE - HALF))
        for ref, matrix in zip((lon_fwd_ref, lon_adj_ref), pair):
            for part, piece in enumerate(split(matrix)):
                for column in range(BLOCK // EDGE):
                    row = EDGE * (column + distance)
                    ref[part, row : row + EDGE, EDGE * column : EDGE * (column + 1)] = piece


def load(ref):
    if ref.shape[0] > 8:
        return ref[...]
    size, groups = ref.shape[1] // 2, HALF // 8
    width = (size - 128) // groups
    return jnp.concatenate(
        [
            jnp.concatenate(
                [ref[:, size * half + width * i : size * half + width * (i + 1)] for half in range(2)],
                axis=1,
            )
            for i in range(groups)
        ],
        axis=0,
    )


def edge_row(ref):
    size = ref.shape[1] // 2
    tiles = [ref[:, size * half - 128 : size * half] for half in (1, 2)]
    return jnp.concatenate([tile[i : i + 1, :] for tile in tiles for i in range(8)], axis=1)


def lat_conv(blocks, matrix_ref):
    high, low = split(jnp.concatenate(blocks, axis=0))
    stacked = jnp.concatenate([high, low], axis=0)
    both = jnp.dot(matrix_ref[...], stacked, preferred_element_type=F32)
    half = both.shape[0] // 2
    return both[:half] + both[half:]


def lon_conv(field, matrix_ref):
    rows, length = field.shape
    count = length // BLOCK
    parts = []
    for part in split(field):
        wide = jnp.concatenate([part[:, -EDGE:], part, part[:, :EDGE]], axis=1)
        parts += [wide[:, BLOCK * i : BLOCK * (i + 1) + 2 * EDGE] for i in range(count)]
    coarse = jnp.dot(jnp.concatenate(parts, axis=0), matrix_ref[0], preferred_element_type=F32)
    fine = jnp.dot(
        jnp.concatenate(parts[:count], axis=0), matrix_ref[1], preferred_element_type=F32
    )
    out = coarse[: count * rows] + coarse[count * rows :] + fine
    return jnp.concatenate([out[rows * i : rows * (i + 1)] for i in range(count)], axis=1)


def seen_kernel(*refs):
    lat_ref, fwd_ref, seen_ref = refs[4:]
    seen_ref[...] = lon_conv(lat_conv([load(ref) for ref in refs[:4]], lat_ref), fwd_ref)


def misfit_kernel(seen_ref, keep_ref, sent_ref, adj_ref, *outs):
    obs = jnp.concatenate([keep_ref[0], sent_ref[0]], axis=0)
    weight = jnp.concatenate([keep_ref[1], sent_ref[1]], axis=0)
    spread = lon_conv(weight * (obs - seen_ref[...]), adj_ref)
    rows, width = outs[0].shape
    lead, trail = lead_trail(spread[:rows], spread[rows:])
    for part, (lead_ref, trail_ref) in enumerate(zip(outs[::2], outs[1::2])):
        columns = slice(width * part, width * (part + 1))
        lead_ref[...] = lead[:, columns]
        trail_ref[...] = trail[:, columns]


def beside(center, above, below):
    width = center.shape[1]
    lateral = pltpu.roll(center, 1, 1) + pltpu.roll(center, width - 1, 1)
    return above + below + lateral


def rim(ref, last):
    if ref.shape[0] > 8:
        return ref[ref.shape[0] - 8 :, :] if last else ref[:8, :]
    size, groups = ref.shape[1] // 2, HALF // 8
    width = (size - 128) // groups
    start = width * (groups - 1) if last else 0
    return jnp.concatenate(
        [ref[:, size * half + start : size * half + start + width] for half in range(2)], axis=1
    )


def prior_kernel(pairs, *refs):
    lead_ref, trail_ref = refs[0], refs[3]
    inside = [load(ref) for ref in refs[1:3]]
    lead_edge, trail_edge = edge_row(refs[4]), edge_row(refs[5])
    out_ref, ext, wide, inner = refs[10:]
    k, y, _ = place()
    rows, length = inside[0].shape
    flip = lax.rem(k, 2) == 1
    north_open = jnp.where(k == 0, 0.0, 1.0)
    south_open = jnp.where(k == pairs - 1, 0.0, 1.0)
    for block, field in enumerate(inside):
        where = 16 + rows * jnp.where(flip, block, 1 - block)
        ext[pl.ds(pl.multiple_of(where, 8), rows), :] = field
    north = jnp.where(flip, rim(lead_ref, True), rim(trail_ref, True))
    south = jnp.where(flip, rim(trail_ref, False), rim(lead_ref, False))
    ext[8:16, :] = north * north_open
    ext[16 + 2 * rows : 24 + 2 * rows, :] = south * south_open
    for block, (left, right) in enumerate(map_pairs(refs[6:10])):
        where = pl.multiple_of(8 + rows * jnp.where(y == 0, block, 1 - block), 8)
        coef = jnp.concatenate([left[0], right[0]], axis=1) + 4.0
        wide[pl.ds(where, rows), :] = coef
    north = jnp.where(flip, lead_edge, trail_edge) + 4.0
    south = jnp.where(flip, trail_edge, lead_edge) + 4.0
    wide[:8, :] = jnp.broadcast_to(north, (8, length))
    wide[8 + 2 * rows :, :] = jnp.broadcast_to(south, (8, length))
    count = 2 * rows + 16
    ext[:8, :] = jnp.zeros((8, length), F32)
    ext[8 + count :, :] = jnp.zeros((8, length), F32)
    center = ext[8 : 8 + count, :]
    around = beside(center, ext[7 : 7 + count, :], ext[9 : 9 + count, :])
    inner[...] = wide[...] * center - around
    inner[:8, :] = inner[:8, :] * north_open
    inner[8 + 2 * rows :, :] = inner[8 + 2 * rows :, :] * south_open
    center = inner[8 : 8 + 2 * rows, :]
    around = beside(center, inner[7 : 7 + 2 * rows, :], inner[9 : 9 + 2 * rows, :])
    outer = wide[8 : 8 + 2 * rows, :] * center - around
    top, bottom = outer[:rows], outer[rows:]
    out_ref[:rows, :] = jnp.where(y == 0, top, bottom)
    out_ref[rows:, :] = jnp.where(y == 0, bottom, top)


def map_pairs(refs):
    return refs[:2], refs[2:]


def adjoint_kernel(*refs):
    refs[5][...] = lat_conv([ref[...] for ref in refs[:4]], refs[4])


def update_kernel(back_ref, prior_ref, *refs):
    rows, width = back_ref.shape[0] // 2, back_ref.shape[1] // 2
    last = back_ref[...] - prior_ref[...]
    sea = [jnp.concatenate([left[1], right[1]], axis=1) for left, right in map_pairs(refs[:4])]
    last_own, last_pair = last[:rows] * sea[0], last[rows:] * sea[1]
    base, states, outs = refs[4:6], refs[6:8], refs[8:]
    for before, state, change in zip(base, states, lead_trail(last_own, last_pair)):
        state[...] = load(before) + change * (1.0 / THETA)
    for i in range(2):
        outs[2 * i][...] = last_own[:, width * i : width * (i + 1)]
        outs[2 * i + 1][...] = last_pair[:, width * i : width * (i + 1)]


def last_kernel(half, *refs):
    lat_ref, prior_ref = refs[4:6]
    rows, width = refs[0].shape
    last = lat_conv([ref[...] for ref in refs[:4]], lat_ref)
    last = last - prior_ref[:, width * half : width * (half + 1)]
    own, pair = map_pairs(refs[6:10])
    refs[10][...] = last[:rows] * own[half][1]
    refs[11][...] = last[rows:] * pair[half][1]


def days_of():
    _, y, c = place()
    return 2 * c + y, 2 * c + (1 - y), 2 * (1 - c) + (1 - y), 2 * (1 - c) + y


def early_kernel(*refs):
    guess_ref, land_ref, fixed_ref, state_ref = refs[4:]
    land = 1.0 - land_ref[...].astype(F32)
    for i, (day, ref) in enumerate(zip(days_of(), refs[:4])):
        guess = guess_ref[day]
        update = (ref[...] - land * guess) * (1.0 / THETA)
        state = guess + update
        fixed_ref[i] = land * state
        state_ref[i] = state + (NEW_RHO * RHO) * update


def final_kernel(half, *refs):
    late, (fixed_ref, sum_ref) = refs[:2], refs[2:4]
    state_ref, last_ref, state, last, sems = refs[-5:]
    days = days_of()[2 * half : 2 * half + 2]
    copies = []
    for i, (day, ref) in enumerate(zip(days, late)):
        last[i] = ref[...] - fixed_ref[2 * half + i]
        state[i] = sum_ref[2 * half + i] + (2.0 * NEW_RHO / DELTA) * last[i]
        for j, (source, target) in enumerate(((state, state_ref), (last, last_ref))):
            copies.append(pltpu.make_async_copy(source.at[i], target.at[day], sems.at[2 * i + j]))
            copies[-1].start()
    for copy in copies:
        copy.wait()


def body(
    pairs,
    first_guess,
    range_coef,
    land_sea,
    lat_kernel,
    lon_kernel,
    observations,
    obs_precision,
    track_counts,
):
    days, rows, width = first_guess.shape
    length = observations.shape[2]
    assert days == 4 and rows == HALF and length == 2 * width and length % BLOCK == 0
    assert width == 8 * 128
    places = [(k, y, c) for k in range(pairs) for y in range(2) for c in range(2)]

    def permute(array, move):
        moves = [(i, places.index(move(*at))) for i, at in enumerate(places)]
        return lax.ppermute(array, AXES, moves)

    def swap(k, y, c, parity):
        target = k + 1 if k % 2 == parity else k - 1
        return (target, y, c) if 0 <= target < pairs else (k, y, 1 - c)

    core = lambda array: permute(array, lambda k, y, c: (k, y, 1 - c))
    pair = lambda array: permute(array, lambda k, y, c: (k, 1 - y, c))
    diag = lambda array: permute(array, lambda k, y, c: (k, 1 - y, 1 - c))
    lead = lambda array: permute(array, lambda k, y, c: swap(k, y, c, 0))
    trail = lambda array: permute(array, lambda k, y, c: swap(k, y, c, 1))

    piece = shape(rows, width)
    packed = shape(8, rows // 8 * width + 128)
    own, to_core, to_pair, to_diag = call(
        pack_kernel,
        [packed] * 4,
        [first_guess, land_sea, range_coef],
        [HBM] * 3,
        scratch=[
            pltpu.VMEM((4, rows, width), F32),
            pltpu.VMEM((rows, width), jnp.int32),
            pltpu.VMEM((8, width), F32),
            pltpu.VMEM((4,) + packed.shape, F32),
            pltpu.SemaphoreType.DMA((10,)),
        ],
        outs=[HBM] * 4,
        vmem=PACK_VMEM,
        name="pack",
    )
    by_pair, by_diag = pair(to_pair), diag(to_diag)
    observations, own = lax.optimization_barrier((observations, own))
    by_core = core(to_core)
    keep, send = call(
        obs_kernel,
        [shape(2, rows, length)] * 2,
        [observations, obs_precision, track_counts[:, :, None]],
        name="observed",
    )
    maps = jnp.stack([range_coef, land_sea.astype(F32)])
    sent = pair(send)
    v_lead, v_trail = call(
        order_kernel,
        [shape(8, 2 * packed.shape[1])] * 2,
        [own, by_pair, by_diag, by_core],
        flops=ADJOINT_COST,
        name="order",
    )
    maps, lat_kernel, v_lead = lax.optimization_barrier((maps, lat_kernel, v_lead))
    lat_fwd, lat_adj, lon_fwd, lon_adj = call(
        functools.partial(matrix_kernel, pairs, rows),
        [shape(4 * rows, 8 * rows, dtype=BF16)] * 2
        + [shape(2, BLOCK + 2 * EDGE, BLOCK, dtype=BF16)] * 2,
        [lat_kernel, lon_kernel],
        [SMEM, SMEM],
        flops=4 * 65 * 2 * 70000,
        name="matrices",
    )
    fields = [lead(v_lead), v_lead, v_trail, trail(v_trail)]
    by_lon = core(maps)
    fields[0], by_lon = lax.optimization_barrier((fields[0], by_lon))
    edges = [fields[0], fields[3]]
    band = shape(rows, length)
    conv = 2 * 3 * 2 * rows * length * 512
    for step in range(2):
        (seen,) = call(
            seen_kernel,
            [shape(2 * rows, length)],
            fields + [lat_fwd, lon_fwd],
            flops=2 * conv,
            name="seen",
        )
        misfit = call(
            misfit_kernel,
            [piece] * 4 if step else [band] * 2,
            [seen, keep, sent, lon_adj],
            flops=conv,
            name="misfit",
        )
        if not step:
            maps, misfit[0] = lax.optimization_barrier((maps, misfit[0]))
            maps_pair = pair(maps)
            maps = [maps, by_lon, maps_pair, core(maps_pair)]
        (prior,) = call(
            functools.partial(prior_kernel, pairs),
            [shape(2 * rows, length)],
            fields + edges + maps,
            scratch=[
                pltpu.VMEM((2 * rows + 32, length), F32),
                pltpu.VMEM((2 * rows + 16, length), F32),
                pltpu.VMEM((2 * rows + 16, length), F32),
            ],
            name="prior",
        )
        common = [lat_adj, prior] + maps
        moved = [lead(m) if i % 2 == 0 else trail(m) for i, m in enumerate(misfit)]
        if not step:
            (back,) = call(
                adjoint_kernel,
                [shape(2 * rows, length)],
                [moved[0], *misfit, moved[1], lat_adj],
                flops=ADJOINT_COST,
                name="adjoint",
            )
            v_lead, v_trail, *pieces = call(
                update_kernel,
                [band] * 2 + [piece] * 4,
                [back, prior, *maps, v_lead, v_trail],
                name="update",
            )
            fields = [lead(v_lead), v_lead, v_trail, trail(v_trail)]
            pieces = [pieces[0], pair(pieces[1]), diag(pieces[3]), core(pieces[2])]
            early = call(
                early_kernel,
                [shape(days, rows, width)] * 2,
                pieces + [first_guess, land_sea],
                name="early",
            )
    moved[0], *early = lax.optimization_barrier((moved[0], *early))
    left_own, left_pair = call(
        functools.partial(last_kernel, 0),
        [piece] * 2,
        [moved[0], *misfit[:2], moved[1], *common],
        flops=LEFT_COST,
        name="update",
    )
    moved[2], left_own = lax.optimization_barrier((moved[2], left_own))
    right_own, right_pair = call(
        functools.partial(last_kernel, 1),
        [piece] * 2,
        [moved[2], *misfit[2:], moved[3], *common],
        flops=conv,
        name="update",
    )
    pieces = [left_own, pair(left_pair), diag(right_pair), core(right_own)]
    result = []
    for half in range(2):
        args = pieces[2 * half : 2 * half + 2] + early
        result = call(
            functools.partial(final_kernel, half),
            [shape(days, rows, width)] * 2,
            args + (result if half else []),
            [VMEM] * 4 + [HBM] * 2 * half,
            outs=[HBM] * 2,
            scratch=[
                pltpu.VMEM((2, rows, width), F32),
                pltpu.VMEM((2, rows, width), F32),
                pltpu.SemaphoreType.DMA((4,)),
            ],
            aliases={4: 0, 5: 1} if half else {},
            flops=0 if half else LEFT_COST,
            name="final",
        )
    return tuple(result)


def solution(mesh):
    assert mesh.shape["lat"] % 2 == 0 and mesh.shape["lon"] == 2
    in_specs = (
        P(None, ("groups", "lat"), "lon"),
        P(("groups", "lat"), "lon"),
        P(("groups", "lat"), "lon"),
        P(),
        P(),
        P("lon", ("groups", "lat"), None),
        P("lon", ("groups", "lat"), None),
        P("lon", ("groups", "lat")),
    )
    out_specs = (P(None, ("groups", "lat"), "lon"), P(None, ("groups", "lat"), "lon"))
    return jax.shard_map(
        functools.partial(body, mesh.shape["lat"] // 2),
        mesh=mesh,
        in_specs=in_specs,
        out_specs=out_specs,
        check_vma=False,
    )
```

```python
import functools

import jax
import jax.numpy as jnp
from jax import lax
from jax.experimental import pallas as pl
from jax.experimental.pallas import tpu as pltpu
from jax.sharding import PartitionSpec as P

HALF = 32
TAPS = 2 * HALF + 1
LOWER = 0.25
UPPER = 120.0
THETA = (LOWER + UPPER) / 2.0
DELTA = (UPPER - LOWER) / 2.0
SIGMA = THETA / DELTA
RHO = 1.0 / SIGMA
NEW_RHO = 1.0 / (2.0 * SIGMA - RHO)
BLOCK = 256
EDGE = 128
LEFT_COST = 5 * 10**9
ADJOINT_COST = 2 * 10**10
PACK_VMEM = 62 * 2**20
AXES = ("lat", "lon")

VMEM = pl.BlockSpec(memory_space=pltpu.VMEM)
SMEM = pl.BlockSpec(memory_space=pltpu.SMEM)
HBM = pl.BlockSpec(memory_space=pltpu.HBM)
F32 = jnp.float32
BF16 = jnp.bfloat16


def place():
    lat = lax.axis_index("lat")
    return lat // 2, lax.rem(lat, 2), lax.axis_index("lon")


def open_sides(pairs):
    k, _, _ = place()
    north, south = jnp.where(k == 0, 0.0, 1.0), jnp.where(k == pairs - 1, 0.0, 1.0)
    flip = lax.rem(k, 2) == 1
    return jnp.where(flip, north, south), jnp.where(flip, south, north)


def lead_trail(own, pair):
    k, y, _ = place()
    straight = lax.rem(k + y, 2) == 1
    return jnp.where(straight, own, pair), jnp.where(straight, pair, own)


def shape(*dims, dtype=F32):
    return jax.ShapeDtypeStruct(dims, dtype)


def call(
    kernel, out_shape, args, specs=None, outs=None, scratch=(), flops=0, vmem=24 * 2**20, aliases=None, name=None
):
    nbytes = 0 if flops == 0 else sum(a.size * a.dtype.itemsize for a in args)
    return list(pl.pallas_call(
        kernel,
        out_shape=out_shape,
        in_specs=specs or [VMEM] * len(args),
        out_specs=outs or [VMEM] * len(out_shape),
        scratch_shapes=list(scratch),
        input_output_aliases=aliases or {},
        compiler_params=pltpu.CompilerParams(vmem_limit_bytes=vmem),
        cost_estimate=pl.CostEstimate(flops=flops, bytes_accessed=nbytes, transcendentals=0),
        name=name,
    )(*args))


def pack_kernel(own, guess_ref, land_ref, coef_ref, first_ref, second_ref, *scratch):
    guess, land, coef, packed, sems = scratch
    _, y, c = place()
    row = y if own else 1 - y
    days = (2 * c + row, 2 * (1 - c) + row)
    rows, width = land.shape
    start = pl.multiple_of((rows - 8) * y, 8)
    copies = [
        pltpu.make_async_copy(land_ref, land, sems.at[0]),
        pltpu.make_async_copy(coef_ref.at[pl.ds(start, 8), :], coef, sems.at[1]),
    ]
    for i, day in enumerate(days):
        copies.append(pltpu.make_async_copy(guess_ref.at[day], guess.at[i], sems.at[2 + i]))
    for copy in copies:
        copy.start()
    copies[0].wait()
    copies[1].wait()
    edge = jnp.where(y == 0, coef[:1, :], coef[7:, :])
    edge = jnp.concatenate([edge[:, i : i + 128] for i in range(0, width, 128)], axis=0)
    outs = []
    for i, ref in enumerate((first_ref, second_ref)):
        copies[2 + i].wait()
        for group in range(rows // 8):
            part = slice(8 * group, 8 * group + 8)
            sea = land[part, :].astype(F32)
            packed[i, :, width * group : width * (group + 1)] = guess[i, part, :] * sea
        packed[i, :, width * (rows // 8) :] = edge
        outs.append(pltpu.make_async_copy(packed.at[i], ref, sems.at[4 + i]))
        outs[-1].start()
    for out in outs:
        out.wait()


def order_kernel(own_ref, pair_ref, diag_ref, core_ref, lead_ref, trail_ref):
    size = own_ref.shape[1]
    for i, (own, pair) in enumerate(((own_ref, pair_ref), (core_ref, diag_ref))):
        lead, trail = lead_trail(own[...], pair[...])
        lead_ref[:, size * i : size * (i + 1)] = lead
        trail_ref[:, size * i : size * (i + 1)] = trail


def obs_kernel(obs_ref, precision_ref, counts_ref, keep_ref, send_ref):
    _, y, c = place()
    width = obs_ref.shape[2] // 2
    for day, ref in ((y, keep_ref), (1 - y, send_ref)):
        counts = counts_ref[day].astype(F32)
        for half, side in ((0, c), (1, 1 - c)):
            source = pl.ds(pl.multiple_of(side * width, width), width)
            target = pl.ds(half * width, width)
            ref[0, :, target] = obs_ref[day, :, source].astype(F32)
            ref[1, :, target] = counts * precision_ref[day, :, source].astype(F32)


def split(values):
    high = values.astype(BF16)
    return high, (values - high.astype(F32)).astype(BF16)


def banded(kern_ref, offset):
    forward = jnp.zeros(offset.shape, F32)
    adjoint = jnp.zeros(offset.shape, F32)
    for tap in range(TAPS):
        hit = offset == tap
        forward = jnp.where(hit, kern_ref[tap], forward)
        adjoint = jnp.where(hit, kern_ref[TAPS - 1 - tap], adjoint)
    return forward, adjoint


def matrix_kernel(pairs, rows, lat_ref, lon_ref, lat_fwd_ref, lat_adj_ref, lon_fwd_ref, lon_adj_ref):
    k, y, _ = place()
    dims = (2 * rows, 4 * rows)

    flip = lax.rem(k, 2) == 1
    out = lax.broadcasted_iota(jnp.int32, dims, 0)
    col = lax.broadcasted_iota(jnp.int32, dims, 1)
    target = rows * jnp.where(y == 0, out // rows, 1 - out // rows) + out % rows
    source = rows * jnp.where(flip, col // rows - 1, 2 - col // rows) + col % rows
    offset = source - target + HALF
    lead_open, trail_open = open_sides(pairs)
    inside = jnp.where(col < 3 * rows, 1.0, trail_open)
    inside = jnp.where(col < rows, lead_open, inside)
    for ref, matrix in zip((lat_fwd_ref, lat_adj_ref), banded(lat_ref, offset)):
        high, low = split(matrix * inside)
        ref[: 2 * rows, : 4 * rows] = high
        ref[: 2 * rows, 4 * rows :] = high
        ref[2 * rows :, : 4 * rows] = low
        ref[2 * rows :, 4 * rows :] = jnp.zeros(dims, BF16)
    dims = (EDGE, EDGE)
    offset = lax.broadcasted_iota(jnp.int32, dims, 0) - lax.broadcasted_iota(jnp.int32, dims, 1)
    for ref in (lon_fwd_ref, lon_adj_ref):
        ref[...] = jnp.zeros(ref.shape, BF16)
    for distance in range(3):
        pair = banded(lon_ref, offset + EDGE * distance - (EDGE - HALF))
        for ref, matrix in zip((lon_fwd_ref, lon_adj_ref), pair):
            for part, piece in enumerate(split(matrix)):
                for column in range(BLOCK // EDGE):
                    row = EDGE * (column + distance)
                    ref[part, row : row + EDGE, EDGE * column : EDGE * (column + 1)] = piece


def load(ref):
    if ref.shape[0] > 8:
        return ref[...]
    size, groups = ref.shape[1] // 2, HALF // 8
    width = (size - 128) // groups
    return jnp.concatenate(
        [
            jnp.concatenate(
                [ref[:, size * half + width * i : size * half + width * (i + 1)] for half in range(2)],
                axis=1,
            )
            for i in range(groups)
        ],
        axis=0,
    )


def edge_row(ref):
    size = ref.shape[1] // 2
    tiles = [ref[:, size * half - 128 : size * half] for half in (1, 2)]
    return jnp.concatenate([tile[i : i + 1, :] for tile in tiles for i in range(8)], axis=1)


def lat_conv(blocks, matrix_ref):
    high, low = split(jnp.concatenate(blocks, axis=0))
    stacked = jnp.concatenate([high, low], axis=0)
    both = jnp.dot(matrix_ref[...], stacked, preferred_element_type=F32)
    half = both.shape[0] // 2
    return both[:half] + both[half:]


def lon_conv(field, matrix_ref):
    rows, length = field.shape
    count = length // BLOCK
    parts = []
    for part in split(field):
        wide = jnp.concatenate([part[:, -EDGE:], part, part[:, :EDGE]], axis=1)
        parts += [wide[:, BLOCK * i : BLOCK * (i + 1) + 2 * EDGE] for i in range(count)]
    coarse = jnp.dot(jnp.concatenate(parts, axis=0), matrix_ref[0], preferred_element_type=F32)
    fine = jnp.dot(
        jnp.concatenate(parts[:count], axis=0), matrix_ref[1], preferred_element_type=F32
    )
    out = coarse[: count * rows] + coarse[count * rows :] + fine
    return jnp.concatenate([out[rows * i : rows * (i + 1)] for i in range(count)], axis=1)


def seen_kernel(*refs):
    lat_ref, fwd_ref, seen_ref = refs[4:]
    seen_ref[...] = lon_conv(lat_conv([load(ref) for ref in refs[:4]], lat_ref), fwd_ref)


def misfit_kernel(seen_ref, keep_ref, sent_ref, adj_ref, *outs):
    obs = jnp.concatenate([keep_ref[0], sent_ref[0]], axis=0)
    weight = jnp.concatenate([keep_ref[1], sent_ref[1]], axis=0)
    spread = lon_conv(weight * (obs - seen_ref[...]), adj_ref)
    rows, width = outs[0].shape
    lead, trail = lead_trail(spread[:rows], spread[rows:])
    for part, (lead_ref, trail_ref) in enumerate(zip(outs[::2], outs[1::2])):
        columns = slice(width * part, width * (part + 1))
        lead_ref[...] = lead[:, columns]
        trail_ref[...] = trail[:, columns]


def beside(center, above, below):
    width = center.shape[1]
    lateral = pltpu.roll(center, 1, 1) + pltpu.roll(center, width - 1, 1)
    return above + below + lateral


def rim(ref, last):
    if ref.shape[0] > 8:
        return ref[ref.shape[0] - 8 :, :] if last else ref[:8, :]
    size, groups = ref.shape[1] // 2, HALF // 8
    width = (size - 128) // groups
    start = width * (groups - 1) if last else 0
    return jnp.concatenate(
        [ref[:, size * half + start : size * half + start + width] for half in range(2)], axis=1
    )


def prior_kernel(pairs, *refs):
    lead_ref, trail_ref = refs[0], refs[3]
    inside = [load(ref) for ref in refs[1:3]]
    lead_edge, trail_edge = edge_row(refs[4]), edge_row(refs[5])
    out_ref, ext, wide, inner = refs[10:]
    k, y, _ = place()
    rows, length = inside[0].shape
    flip = lax.rem(k, 2) == 1
    north_open = jnp.where(k == 0, 0.0, 1.0)
    south_open = jnp.where(k == pairs - 1, 0.0, 1.0)
    for block, field in enumerate(inside):
        where = 16 + rows * jnp.where(flip, block, 1 - block)
        ext[pl.ds(pl.multiple_of(where, 8), rows), :] = field
    north = jnp.where(flip, rim(lead_ref, True), rim(trail_ref, True))
    south = jnp.where(flip, rim(trail_ref, False), rim(lead_ref, False))
    ext[8:16, :] = north * north_open
    ext[16 + 2 * rows : 24 + 2 * rows, :] = south * south_open
    for block, (left, right) in enumerate(map_pairs(refs[6:10])):
        where = pl.multiple_of(8 + rows * jnp.where(y == 0, block, 1 - block), 8)
        coef = jnp.concatenate([left[0], right[0]], axis=1) + 4.0
        wide[pl.ds(where, rows), :] = coef
    north = jnp.where(flip, lead_edge, trail_edge) + 4.0
    south = jnp.where(flip, trail_edge, lead_edge) + 4.0
    wide[:8, :] = jnp.broadcast_to(north, (8, length))
    wide[8 + 2 * rows :, :] = jnp.broadcast_to(south, (8, length))
    count = 2 * rows + 16
    ext[:8, :] = jnp.zeros((8, length), F32)
    ext[8 + count :, :] = jnp.zeros((8, length), F32)
    center = ext[8 : 8 + count, :]
    around = beside(center, ext[7 : 7 + count, :], ext[9 : 9 + count, :])
    inner[...] = wide[...] * center - around
    inner[:8, :] = inner[:8, :] * north_open
    inner[8 + 2 * rows :, :] = inner[8 + 2 * rows :, :] * south_open
    center = inner[8 : 8 + 2 * rows, :]
    around = beside(center, inner[7 : 7 + 2 * rows, :], inner[9 : 9 + 2 * rows, :])
    outer = wide[8 : 8 + 2 * rows, :] * center - around
    top, bottom = outer[:rows], outer[rows:]
    out_ref[:rows, :] = jnp.where(y == 0, top, bottom)
    out_ref[rows:, :] = jnp.where(y == 0, bottom, top)


def map_pairs(refs):
    return refs[:2], refs[2:]


def adjoint_kernel(*refs):
    refs[5][...] = lat_conv([ref[...] for ref in refs[:4]], refs[4])


def update_kernel(back_ref, prior_ref, *refs):
    rows, width = back_ref.shape[0] // 2, back_ref.shape[1] // 2
    last = back_ref[...] - prior_ref[...]
    sea = [jnp.concatenate([left[1], right[1]], axis=1) for left, right in map_pairs(refs[:4])]
    last_own, last_pair = last[:rows] * sea[0], last[rows:] * sea[1]
    base, states, outs = refs[4:6], refs[6:8], refs[8:]
    for before, state, change in zip(base, states, lead_trail(last_own, last_pair)):
        state[...] = load(before) + change * (1.0 / THETA)
    for i in range(2):
        outs[2 * i][...] = last_own[:, width * i : width * (i + 1)]
        outs[2 * i + 1][...] = last_pair[:, width * i : width * (i + 1)]


def last_kernel(half, *refs):
    lat_ref, prior_ref = refs[4:6]
    rows, width = refs[0].shape
    last = lat_conv([ref[...] for ref in refs[:4]], lat_ref)
    last = last - prior_ref[:, width * half : width * (half + 1)]
    own, pair = map_pairs(refs[6:10])
    refs[10][...] = last[:rows] * own[half][1]
    refs[11][...] = last[rows:] * pair[half][1]


def days_of():
    _, y, c = place()
    return 2 * c + y, 2 * c + (1 - y), 2 * (1 - c) + (1 - y), 2 * (1 - c) + y


def early_kernel(*refs):
    guess_ref, land_ref, fixed_ref, state_ref = refs[4:]
    land = 1.0 - land_ref[...].astype(F32)
    for i, (day, ref) in enumerate(zip(days_of(), refs[:4])):
        guess = guess_ref[day]
        update = (ref[...] - land * guess) * (1.0 / THETA)
        state = guess + update
        fixed_ref[i] = land * state
        state_ref[i] = state + (NEW_RHO * RHO) * update


def final_kernel(half, *refs):
    late, (fixed_ref, sum_ref) = refs[:2], refs[2:4]
    state_ref, last_ref, state, last, sems = refs[-5:]
    days = days_of()[2 * half : 2 * half + 2]
    copies = []
    for i, (day, ref) in enumerate(zip(days, late)):
        last[i] = ref[...] - fixed_ref[2 * half + i]
        state[i] = sum_ref[2 * half + i] + (2.0 * NEW_RHO / DELTA) * last[i]
        for j, (source, target) in enumerate(((state, state_ref), (last, last_ref))):
            copies.append(pltpu.make_async_copy(source.at[i], target.at[day], sems.at[2 * i + j]))
            copies[-1].start()
    for copy in copies:
        copy.wait()


def body(
    pairs,
    first_guess,
    range_coef,
    land_sea,
    lat_kernel,
    lon_kernel,
    observations,
    obs_precision,
    track_counts,
):
    days, rows, width = first_guess.shape
    length = observations.shape[2]
    assert days == 4 and rows == HALF and length == 2 * width and length % BLOCK == 0
    assert width == 8 * 128
    places = [(k, y, c) for k in range(pairs) for y in range(2) for c in range(2)]

    def permute(array, move):
        moves = [(i, places.index(move(*at))) for i, at in enumerate(places)]
        return lax.ppermute(array, AXES, moves)

    def swap(k, y, c, parity):
        target = k + 1 if k % 2 == parity else k - 1
        return (target, y, c) if 0 <= target < pairs else (k, y, 1 - c)

    core = lambda array: permute(array, lambda k, y, c: (k, y, 1 - c))
    pair = lambda array: permute(array, lambda k, y, c: (k, 1 - y, c))
    diag = lambda array: permute(array, lambda k, y, c: (k, 1 - y, 1 - c))
    lead = lambda array: permute(array, lambda k, y, c: swap(k, y, c, 0))
    trail = lambda array: permute(array, lambda k, y, c: swap(k, y, c, 1))

    piece = shape(rows, width)
    packed = shape(8, rows // 8 * width + 128)
    def pack(is_own, land):
        return call(
            functools.partial(pack_kernel, is_own),
            [packed] * 2,
            [first_guess, land, range_coef],
            [HBM] * 3,
            outs=[HBM] * 2,
            scratch=[
                pltpu.VMEM((2, rows, width), F32),
                pltpu.VMEM((rows, width), jnp.int32),
                pltpu.VMEM((8, width), F32),
                pltpu.VMEM((2,) + packed.shape, F32),
                pltpu.SemaphoreType.DMA((6,)),
            ],
            vmem=PACK_VMEM,
            name="pack",
        )

    to_pair, to_diag = pack(False, land_sea)
    land, to_pair = lax.optimization_barrier((land_sea, to_pair))
    own, to_core = pack(True, land)
    by_pair, by_diag = pair(to_pair), diag(to_diag)
    observations, own = lax.optimization_barrier((observations, own))
    by_core = core(to_core)
    keep, send = call(
        obs_kernel,
        [shape(2, rows, length)] * 2,
        [observations, obs_precision, track_counts[:, :, None]],
        name="observed",
    )
    maps = jnp.stack([range_coef, land_sea.astype(F32)])
    sent = pair(send)
    v_lead, v_trail = call(
        order_kernel,
        [shape(8, 2 * packed.shape[1])] * 2,
        [own, by_pair, by_diag, by_core],
        flops=ADJOINT_COST,
        name="order",
    )
    maps, lat_kernel, v_lead = lax.optimization_barrier((maps, lat_kernel, v_lead))
    lat_fwd, lat_adj, lon_fwd, lon_adj = call(
        functools.partial(matrix_kernel, pairs, rows),
        [shape(4 * rows, 8 * rows, dtype=BF16)] * 2
        + [shape(2, BLOCK + 2 * EDGE, BLOCK, dtype=BF16)] * 2,
        [lat_kernel, lon_kernel],
        [SMEM, SMEM],
        flops=4 * 65 * 2 * 70000,
        name="matrices",
    )
    fields = [lead(v_lead), v_lead, v_trail, trail(v_trail)]
    by_lon = core(maps)
    fields[0], by_lon = lax.optimization_barrier((fields[0], by_lon))
    edges = [fields[0], fields[3]]
    band = shape(rows, length)
    conv = 2 * 3 * 2 * rows * length * 512
    for step in range(2):
        (seen,) = call(
            seen_kernel,
            [shape(2 * rows, length)],
            fields + [lat_fwd, lon_fwd],
            flops=2 * conv,
            name="seen",
        )
        misfit = call(
            misfit_kernel,
            [piece] * 4 if step else [band] * 2,
            [seen, keep, sent, lon_adj],
            flops=conv,
            name="misfit",
        )
        if not step:
            maps, misfit[0] = lax.optimization_barrier((maps, misfit[0]))
            maps_pair = pair(maps)
            maps = [maps, by_lon, maps_pair, core(maps_pair)]
        (prior,) = call(
            functools.partial(prior_kernel, pairs),
            [shape(2 * rows, length)],
            fields + edges + maps,
            scratch=[
                pltpu.VMEM((2 * rows + 32, length), F32),
                pltpu.VMEM((2 * rows + 16, length), F32),
                pltpu.VMEM((2 * rows + 16, length), F32),
            ],
            name="prior",
        )
        common = [lat_adj, prior] + maps
        moved = [lead(m) if i % 2 == 0 else trail(m) for i, m in enumerate(misfit)]
        if not step:
            (back,) = call(
                adjoint_kernel,
                [shape(2 * rows, length)],
                [moved[0], *misfit, moved[1], lat_adj],
                flops=ADJOINT_COST,
                name="adjoint",
            )
            v_lead, v_trail, *pieces = call(
                update_kernel,
                [band] * 2 + [piece] * 4,
                [back, prior, *maps, v_lead, v_trail],
                name="update",
            )
            fields = [lead(v_lead), v_lead, v_trail, trail(v_trail)]
            pieces = [pieces[0], pair(pieces[1]), diag(pieces[3]), core(pieces[2])]
            early = call(
                early_kernel,
                [shape(days, rows, width)] * 2,
                pieces + [first_guess, land_sea],
                name="early",
            )
    moved[0], *early = lax.optimization_barrier((moved[0], *early))
    left_own, left_pair = call(
        functools.partial(last_kernel, 0),
        [piece] * 2,
        [moved[0], *misfit[:2], moved[1], *common],
        flops=LEFT_COST,
        name="update",
    )
    moved[2], left_own = lax.optimization_barrier((moved[2], left_own))
    right_own, right_pair = call(
        functools.partial(last_kernel, 1),
        [piece] * 2,
        [moved[2], *misfit[2:], moved[3], *common],
        flops=conv,
        name="update",
    )
    pieces = [left_own, pair(left_pair), diag(right_pair), core(right_own)]
    result = []
    for half in range(2):
        args = pieces[2 * half : 2 * half + 2] + early
        result = call(
            functools.partial(final_kernel, half),
            [shape(days, rows, width)] * 2,
            args + (result if half else []),
            [VMEM] * 4 + [HBM] * 2 * half,
            outs=[HBM] * 2,
            scratch=[
                pltpu.VMEM((2, rows, width), F32),
                pltpu.VMEM((2, rows, width), F32),
                pltpu.SemaphoreType.DMA((4,)),
            ],
            aliases={4: 0, 5: 1} if half else {},
            flops=0 if half else LEFT_COST,
            name="final",
        )
    return tuple(result)


def solution(mesh):
    assert mesh.shape["lat"] % 2 == 0 and mesh.shape["lon"] == 2
    in_specs = (
        P(None, ("groups", "lat"), "lon"),
        P(("groups", "lat"), "lon"),
        P(("groups", "lat"), "lon"),
        P(),
        P(),
        P("lon", ("groups", "lat"), None),
        P("lon", ("groups", "lat"), None),
        P("lon", ("groups", "lat")),
    )
    out_specs = (P(None, ("groups", "lat"), "lon"), P(None, ("groups", "lat"), "lon"))
    return jax.shard_map(
        functools.partial(body, mesh.shape["lat"] // 2),
        mesh=mesh,
        in_specs=in_specs,
        out_specs=out_specs,
        check_vma=False,
    )
```

```python
import functools

import jax
import jax.numpy as jnp
from jax import lax
from jax.experimental import pallas as pl
from jax.experimental.pallas import tpu as pltpu
from jax.sharding import PartitionSpec as P

HALF = 32
TAPS = 2 * HALF + 1
LOWER = 0.25
UPPER = 120.0
THETA = (LOWER + UPPER) / 2.0
DELTA = (UPPER - LOWER) / 2.0
SIGMA = THETA / DELTA
RHO = 1.0 / SIGMA
NEW_RHO = 1.0 / (2.0 * SIGMA - RHO)
BLOCK = 256
EDGE = 128
LEFT_COST = 5 * 10**9
ADJOINT_COST = 2 * 10**10
PACK_VMEM = 62 * 2**20
AXES = ("lat", "lon")

VMEM = pl.BlockSpec(memory_space=pltpu.VMEM)
SMEM = pl.BlockSpec(memory_space=pltpu.SMEM)
HBM = pl.BlockSpec(memory_space=pltpu.HBM)
F32 = jnp.float32
BF16 = jnp.bfloat16


def place():
    lat = lax.axis_index("lat")
    return lat // 2, lax.rem(lat, 2), lax.axis_index("lon")


def open_sides(pairs):
    k, y, _ = place()
    north, south = jnp.where(k == 0, 0.0, 1.0), jnp.where(k == pairs - 1, 0.0, 1.0)
    flip = lax.rem(k + y, 2) == 1
    return jnp.where(flip, north, south), jnp.where(flip, south, north)


def lead_trail(own, pair):
    k, y, _ = place()
    straight = lax.rem(k, 2) == 1
    return jnp.where(straight, own, pair), jnp.where(straight, pair, own)


def shape(*dims, dtype=F32):
    return jax.ShapeDtypeStruct(dims, dtype)


def call(
    kernel, out_shape, args, specs=None, outs=None, scratch=(), flops=0, vmem=24 * 2**20, aliases=None, name=None
):
    nbytes = 0 if flops == 0 else sum(a.size * a.dtype.itemsize for a in args)
    return list(pl.pallas_call(
        kernel,
        out_shape=out_shape,
        in_specs=specs or [VMEM] * len(args),
        out_specs=outs or [VMEM] * len(out_shape),
        scratch_shapes=list(scratch),
        input_output_aliases=aliases or {},
        compiler_params=pltpu.CompilerParams(vmem_limit_bytes=vmem),
        cost_estimate=pl.CostEstimate(flops=flops, bytes_accessed=nbytes, transcendentals=0),
        name=name,
    )(*args))


def pack_kernel(own, guess_ref, land_ref, coef_ref, first_ref, second_ref, *scratch):
    guess, land, coef, packed, sems = scratch
    _, y, c = place()
    row = y if own else 1 - y
    days = (2 * c + row, 2 * (1 - c) + row)
    rows, width = land.shape
    start = pl.multiple_of((rows - 8) * y, 8)
    copies = [
        pltpu.make_async_copy(land_ref, land, sems.at[0]),
        pltpu.make_async_copy(coef_ref.at[pl.ds(start, 8), :], coef, sems.at[1]),
    ]
    for i, day in enumerate(days):
        copies.append(pltpu.make_async_copy(guess_ref.at[day], guess.at[i], sems.at[2 + i]))
    for copy in copies:
        copy.start()
    copies[0].wait()
    copies[1].wait()
    edge = jnp.where(y == 0, coef[:1, :], coef[7:, :])
    edge = jnp.concatenate([edge[:, i : i + 128] for i in range(0, width, 128)], axis=0)
    outs = []
    for i, ref in enumerate((first_ref, second_ref)):
        copies[2 + i].wait()
        for group in range(rows // 8):
            part = slice(8 * group, 8 * group + 8)
            sea = land[part, :].astype(F32)
            packed[i, :, width * group : width * (group + 1)] = guess[i, part, :] * sea
        packed[i, :, width * (rows // 8) :] = edge
        outs.append(pltpu.make_async_copy(packed.at[i], ref, sems.at[4 + i]))
        outs[-1].start()
    for out in outs:
        out.wait()


def order_kernel(own_ref, pair_ref, diag_ref, core_ref, lead_ref, trail_ref):
    size = own_ref.shape[1]
    for i, (own, pair) in enumerate(((own_ref, pair_ref), (core_ref, diag_ref))):
        lead, trail = lead_trail(own[...], pair[...])
        lead_ref[:, size * i : size * (i + 1)] = lead
        trail_ref[:, size * i : size * (i + 1)] = trail


def obs_kernel(obs_ref, precision_ref, counts_ref, keep_ref, send_ref):
    _, y, c = place()
    width = obs_ref.shape[2] // 2
    for day, ref in ((y, keep_ref), (1 - y, send_ref)):
        counts = counts_ref[day].astype(F32)
        for half, side in ((0, c), (1, 1 - c)):
            source = pl.ds(pl.multiple_of(side * width, width), width)
            target = pl.ds(half * width, width)
            ref[0, :, target] = obs_ref[day, :, source].astype(F32)
            ref[1, :, target] = counts * precision_ref[day, :, source].astype(F32)


def split(values):
    high = values.astype(BF16)
    return high, (values - high.astype(F32)).astype(BF16)


def banded(kern_ref, offset):
    forward = jnp.zeros(offset.shape, F32)
    adjoint = jnp.zeros(offset.shape, F32)
    for tap in range(TAPS):
        hit = offset == tap
        forward = jnp.where(hit, kern_ref[tap], forward)
        adjoint = jnp.where(hit, kern_ref[TAPS - 1 - tap], adjoint)
    return forward, adjoint


def matrix_kernel(pairs, rows, lat_ref, lon_ref, lat_fwd_ref, lat_adj_ref, lon_fwd_ref, lon_adj_ref):
    k, y, _ = place()
    dims = (2 * rows, 4 * rows)

    flip = lax.rem(k + y, 2) == 1
    out = lax.broadcasted_iota(jnp.int32, dims, 0)
    col = lax.broadcasted_iota(jnp.int32, dims, 1)
    target = rows * jnp.where(y == 0, out // rows, 1 - out // rows) + out % rows
    source = rows * jnp.where(flip, col // rows - 1, 2 - col // rows) + col % rows
    offset = source - target + HALF
    lead_open, trail_open = open_sides(pairs)
    inside = jnp.where(col < 3 * rows, 1.0, trail_open)
    inside = jnp.where(col < rows, lead_open, inside)
    for ref, matrix in zip((lat_fwd_ref, lat_adj_ref), banded(lat_ref, offset)):
        high, low = split(matrix * inside)
        ref[: 2 * rows, : 4 * rows] = high
        ref[: 2 * rows, 4 * rows :] = high
        ref[2 * rows :, : 4 * rows] = low
        ref[2 * rows :, 4 * rows :] = jnp.zeros(dims, BF16)
    dims = (EDGE, EDGE)
    offset = lax.broadcasted_iota(jnp.int32, dims, 0) - lax.broadcasted_iota(jnp.int32, dims, 1)
    for ref in (lon_fwd_ref, lon_adj_ref):
        ref[...] = jnp.zeros(ref.shape, BF16)
    for distance in range(3):
        pair = banded(lon_ref, offset + EDGE * distance - (EDGE - HALF))
        for ref, matrix in zip((lon_fwd_ref, lon_adj_ref), pair):
            for part, piece in enumerate(split(matrix)):
                for column in range(BLOCK // EDGE):
                    row = EDGE * (column + distance)
                    ref[part, row : row + EDGE, EDGE * column : EDGE * (column + 1)] = piece


def load(ref):
    if ref.shape[0] > 8:
        return ref[...]
    size, groups = ref.shape[1] // 2, HALF // 8
    width = (size - 128) // groups
    return jnp.concatenate(
        [
            jnp.concatenate(
                [ref[:, size * half + width * i : size * half + width * (i + 1)] for half in range(2)],
                axis=1,
            )
            for i in range(groups)
        ],
        axis=0,
    )


def edge_row(ref):
    size = ref.shape[1] // 2
    tiles = [ref[:, size * half - 128 : size * half] for half in (1, 2)]
    return jnp.concatenate([tile[i : i + 1, :] for tile in tiles for i in range(8)], axis=1)


def lat_conv(blocks, matrix_ref):
    high, low = split(jnp.concatenate(blocks, axis=0))
    stacked = jnp.concatenate([high, low], axis=0)
    both = jnp.dot(matrix_ref[...], stacked, preferred_element_type=F32)
    half = both.shape[0] // 2
    return both[:half] + both[half:]


def lon_conv(field, matrix_ref):
    rows, length = field.shape
    count = length // BLOCK
    parts = []
    for part in split(field):
        wide = jnp.concatenate([part[:, -EDGE:], part, part[:, :EDGE]], axis=1)
        parts += [wide[:, BLOCK * i : BLOCK * (i + 1) + 2 * EDGE] for i in range(count)]
    coarse = jnp.dot(jnp.concatenate(parts, axis=0), matrix_ref[0], preferred_element_type=F32)
    fine = jnp.dot(
        jnp.concatenate(parts[:count], axis=0), matrix_ref[1], preferred_element_type=F32
    )
    out = coarse[: count * rows] + coarse[count * rows :] + fine
    return jnp.concatenate([out[rows * i : rows * (i + 1)] for i in range(count)], axis=1)


def seen_kernel(*refs):
    lat_ref, fwd_ref, seen_ref = refs[4:]
    seen_ref[...] = lon_conv(lat_conv([load(ref) for ref in refs[:4]], lat_ref), fwd_ref)


def misfit_kernel(seen_ref, keep_ref, sent_ref, adj_ref, *outs):
    obs = jnp.concatenate([keep_ref[0], sent_ref[0]], axis=0)
    weight = jnp.concatenate([keep_ref[1], sent_ref[1]], axis=0)
    spread = lon_conv(weight * (obs - seen_ref[...]), adj_ref)
    rows, width = outs[0].shape
    lead, trail = lead_trail(spread[:rows], spread[rows:])
    for part, (lead_ref, trail_ref) in enumerate(zip(outs[::2], outs[1::2])):
        columns = slice(width * part, width * (part + 1))
        lead_ref[...] = lead[:, columns]
        trail_ref[...] = trail[:, columns]


def beside(center, above, below):
    width = center.shape[1]
    lateral = pltpu.roll(center, 1, 1) + pltpu.roll(center, width - 1, 1)
    return above + below + lateral


def rim(ref, last):
    if ref.shape[0] > 8:
        return ref[ref.shape[0] - 8 :, :] if last else ref[:8, :]
    size, groups = ref.shape[1] // 2, HALF // 8
    width = (size - 128) // groups
    start = width * (groups - 1) if last else 0
    return jnp.concatenate(
        [ref[:, size * half + start : size * half + start + width] for half in range(2)], axis=1
    )


def prior_kernel(pairs, *refs):
    lead_ref, trail_ref = refs[0], refs[3]
    inside = [load(ref) for ref in refs[1:3]]
    lead_edge, trail_edge = edge_row(refs[4]), edge_row(refs[5])
    out_ref, ext, wide, inner = refs[10:]
    k, y, _ = place()
    rows, length = inside[0].shape
    flip = lax.rem(k + y, 2) == 1
    north_open = jnp.where(k == 0, 0.0, 1.0)
    south_open = jnp.where(k == pairs - 1, 0.0, 1.0)
    for block, field in enumerate(inside):
        where = 16 + rows * jnp.where(flip, block, 1 - block)
        ext[pl.ds(pl.multiple_of(where, 8), rows), :] = field
    north = jnp.where(flip, rim(lead_ref, True), rim(trail_ref, True))
    south = jnp.where(flip, rim(trail_ref, False), rim(lead_ref, False))
    ext[8:16, :] = north * north_open
    ext[16 + 2 * rows : 24 + 2 * rows, :] = south * south_open
    for block, (left, right) in enumerate(map_pairs(refs[6:10])):
        where = pl.multiple_of(8 + rows * jnp.where(y == 0, block, 1 - block), 8)
        coef = jnp.concatenate([left[0], right[0]], axis=1) + 4.0
        wide[pl.ds(where, rows), :] = coef
    north = jnp.where(flip, lead_edge, trail_edge) + 4.0
    south = jnp.where(flip, trail_edge, lead_edge) + 4.0
    wide[:8, :] = jnp.broadcast_to(north, (8, length))
    wide[8 + 2 * rows :, :] = jnp.broadcast_to(south, (8, length))
    count = 2 * rows + 16
    ext[:8, :] = jnp.zeros((8, length), F32)
    ext[8 + count :, :] = jnp.zeros((8, length), F32)
    center = ext[8 : 8 + count, :]
    around = beside(center, ext[7 : 7 + count, :], ext[9 : 9 + count, :])
    inner[...] = wide[...] * center - around
    inner[:8, :] = inner[:8, :] * north_open
    inner[8 + 2 * rows :, :] = inner[8 + 2 * rows :, :] * south_open
    center = inner[8 : 8 + 2 * rows, :]
    around = beside(center, inner[7 : 7 + 2 * rows, :], inner[9 : 9 + 2 * rows, :])
    outer = wide[8 : 8 + 2 * rows, :] * center - around
    top, bottom = outer[:rows], outer[rows:]
    out_ref[:rows, :] = jnp.where(y == 0, top, bottom)
    out_ref[rows:, :] = jnp.where(y == 0, bottom, top)


def map_pairs(refs):
    return refs[:2], refs[2:]


def adjoint_kernel(*refs):
    refs[5][...] = lat_conv([ref[...] for ref in refs[:4]], refs[4])


def update_kernel(back_ref, prior_ref, *refs):
    rows, width = back_ref.shape[0] // 2, back_ref.shape[1] // 2
    last = back_ref[...] - prior_ref[...]
    sea = [jnp.concatenate([left[1], right[1]], axis=1) for left, right in map_pairs(refs[:4])]
    last_own, last_pair = last[:rows] * sea[0], last[rows:] * sea[1]
    base, states, outs = refs[4:6], refs[6:8], refs[8:]
    for before, state, change in zip(base, states, lead_trail(last_own, last_pair)):
        state[...] = load(before) + change * (1.0 / THETA)
    for i in range(2):
        outs[2 * i][...] = last_own[:, width * i : width * (i + 1)]
        outs[2 * i + 1][...] = last_pair[:, width * i : width * (i + 1)]


def last_kernel(half, *refs):
    lat_ref, prior_ref = refs[4:6]
    rows, width = refs[0].shape
    last = lat_conv([ref[...] for ref in refs[:4]], lat_ref)
    last = last - prior_ref[:, width * half : width * (half + 1)]
    own, pair = map_pairs(refs[6:10])
    refs[10][...] = last[:rows] * own[half][1]
    refs[11][...] = last[rows:] * pair[half][1]


def days_of():
    _, y, c = place()
    return 2 * c + y, 2 * c + (1 - y), 2 * (1 - c) + (1 - y), 2 * (1 - c) + y


def early_kernel(*refs):
    guess_ref, land_ref, fixed_ref, state_ref = refs[4:]
    land = 1.0 - land_ref[...].astype(F32)
    for i, (day, ref) in enumerate(zip(days_of(), refs[:4])):
        guess = guess_ref[day]
        update = (ref[...] - land * guess) * (1.0 / THETA)
        state = guess + update
        fixed_ref[i] = land * state
        state_ref[i] = state + (NEW_RHO * RHO) * update


def final_kernel(half, *refs):
    late, (fixed_ref, sum_ref) = refs[:2], refs[2:4]
    state_ref, last_ref, state, last, sems = refs[-5:]
    days = days_of()[2 * half : 2 * half + 2]
    copies = []
    for i, (day, ref) in enumerate(zip(days, late)):
        last[i] = ref[...] - fixed_ref[2 * half + i]
        state[i] = sum_ref[2 * half + i] + (2.0 * NEW_RHO / DELTA) * last[i]
        for j, (source, target) in enumerate(((state, state_ref), (last, last_ref))):
            copies.append(pltpu.make_async_copy(source.at[i], target.at[day], sems.at[2 * i + j]))
            copies[-1].start()
    for copy in copies:
        copy.wait()


def body(
    pairs,
    first_guess,
    range_coef,
    land_sea,
    lat_kernel,
    lon_kernel,
    observations,
    obs_precision,
    track_counts,
):
    days, rows, width = first_guess.shape
    length = observations.shape[2]
    assert days == 4 and rows == HALF and length == 2 * width and length % BLOCK == 0
    assert width == 8 * 128
    places = [(k, y, c) for k in range(pairs) for y in range(2) for c in range(2)]

    def permute(array, move):
        moves = [(i, places.index(move(*at))) for i, at in enumerate(places)]
        return lax.ppermute(array, AXES, moves)

    def swap(k, y, c, parity):
        target = k + 1 if (k + y) % 2 == parity else k - 1
        return (target, y, c) if 0 <= target < pairs else (k, y, 1 - c)

    core = lambda array: permute(array, lambda k, y, c: (k, y, 1 - c))
    pair = lambda array: permute(array, lambda k, y, c: (k, 1 - y, c))
    diag = lambda array: permute(array, lambda k, y, c: (k, 1 - y, 1 - c))
    lead = lambda array: permute(array, lambda k, y, c: swap(k, y, c, 0))
    trail = lambda array: permute(array, lambda k, y, c: swap(k, y, c, 1))

    piece = shape(rows, width)
    packed = shape(8, rows // 8 * width + 128)
    def pack(is_own, land):
        return call(
            functools.partial(pack_kernel, is_own),
            [packed] * 2,
            [first_guess, land, range_coef],
            [HBM] * 3,
            outs=[HBM] * 2,
            scratch=[
                pltpu.VMEM((2, rows, width), F32),
                pltpu.VMEM((rows, width), jnp.int32),
                pltpu.VMEM((8, width), F32),
                pltpu.VMEM((2,) + packed.shape, F32),
                pltpu.SemaphoreType.DMA((6,)),
            ],
            vmem=PACK_VMEM,
            name="pack",
        )

    to_pair, to_diag = pack(False, land_sea)
    land, to_pair = lax.optimization_barrier((land_sea, to_pair))
    own, to_core = pack(True, land)
    by_pair, by_diag = pair(to_pair), diag(to_diag)
    observations, own = lax.optimization_barrier((observations, own))
    by_core = core(to_core)
    keep, send = call(
        obs_kernel,
        [shape(2, rows, length)] * 2,
        [observations, obs_precision, track_counts[:, :, None]],
        name="observed",
    )
    maps = jnp.stack([range_coef, land_sea.astype(F32)])
    sent = pair(send)
    v_lead, v_trail = call(
        order_kernel,
        [shape(8, 2 * packed.shape[1])] * 2,
        [own, by_pair, by_diag, by_core],
        flops=ADJOINT_COST,
        name="order",
    )
    maps, lat_kernel, v_lead = lax.optimization_barrier((maps, lat_kernel, v_lead))
    lat_fwd, lat_adj, lon_fwd, lon_adj = call(
        functools.partial(matrix_kernel, pairs, rows),
        [shape(4 * rows, 8 * rows, dtype=BF16)] * 2
        + [shape(2, BLOCK + 2 * EDGE, BLOCK, dtype=BF16)] * 2,
        [lat_kernel, lon_kernel],
        [SMEM, SMEM],
        flops=4 * 65 * 2 * 70000,
        name="matrices",
    )
    fields = [lead(v_lead), v_lead, v_trail, trail(v_trail)]
    by_lon = core(maps)
    fields[0], by_lon = lax.optimization_barrier((fields[0], by_lon))
    edges = [fields[0], fields[3]]
    band = shape(rows, length)
    conv = 2 * 3 * 2 * rows * length * 512
    for step in range(2):
        (seen,) = call(
            seen_kernel,
            [shape(2 * rows, length)],
            fields + [lat_fwd, lon_fwd],
            flops=2 * conv,
            name="seen",
        )
        misfit = call(
            misfit_kernel,
            [piece] * 4 if step else [band] * 2,
            [seen, keep, sent, lon_adj],
            flops=conv,
            name="misfit",
        )
        if not step:
            maps, misfit[0] = lax.optimization_barrier((maps, misfit[0]))
            maps_pair = pair(maps)
            maps = [maps, by_lon, maps_pair, core(maps_pair)]
        (prior,) = call(
            functools.partial(prior_kernel, pairs),
            [shape(2 * rows, length)],
            fields + edges + maps,
            scratch=[
                pltpu.VMEM((2 * rows + 32, length), F32),
                pltpu.VMEM((2 * rows + 16, length), F32),
                pltpu.VMEM((2 * rows + 16, length), F32),
            ],
            name="prior",
        )
        common = [lat_adj, prior] + maps
        moved = [lead(m) if i % 2 == 0 else trail(m) for i, m in enumerate(misfit)]
        if not step:
            (back,) = call(
                adjoint_kernel,
                [shape(2 * rows, length)],
                [moved[0], *misfit, moved[1], lat_adj],
                flops=ADJOINT_COST,
                name="adjoint",
            )
            v_lead, v_trail, *pieces = call(
                update_kernel,
                [band] * 2 + [piece] * 4,
                [back, prior, *maps, v_lead, v_trail],
                name="update",
            )
            fields = [lead(v_lead), v_lead, v_trail, trail(v_trail)]
            pieces = [pieces[0], pair(pieces[1]), diag(pieces[3]), core(pieces[2])]
            early = call(
                early_kernel,
                [shape(days, rows, width)] * 2,
                pieces + [first_guess, land_sea],
                name="early",
            )
    moved[0], *early = lax.optimization_barrier((moved[0], *early))
    left_own, left_pair = call(
        functools.partial(last_kernel, 0),
        [piece] * 2,
        [moved[0], *misfit[:2], moved[1], *common],
        flops=LEFT_COST,
        name="update",
    )
    moved[2], left_own = lax.optimization_barrier((moved[2], left_own))
    right_own, right_pair = call(
        functools.partial(last_kernel, 1),
        [piece] * 2,
        [moved[2], *misfit[2:], moved[3], *common],
        flops=conv,
        name="update",
    )
    pieces = [left_own, pair(left_pair), diag(right_pair), core(right_own)]
    result = []
    for half in range(2):
        args = pieces[2 * half : 2 * half + 2] + early
        result = call(
            functools.partial(final_kernel, half),
            [shape(days, rows, width)] * 2,
            args + (result if half else []),
            [VMEM] * 4 + [HBM] * 2 * half,
            outs=[HBM] * 2,
            scratch=[
                pltpu.VMEM((2, rows, width), F32),
                pltpu.VMEM((2, rows, width), F32),
                pltpu.SemaphoreType.DMA((4,)),
            ],
            aliases={4: 0, 5: 1} if half else {},
            flops=0 if half else LEFT_COST,
            name="final",
        )
    return tuple(result)


def solution(mesh):
    assert mesh.shape["lat"] % 2 == 0 and mesh.shape["lon"] == 2
    in_specs = (
        P(None, ("groups", "lat"), "lon"),
        P(("groups", "lat"), "lon"),
        P(("groups", "lat"), "lon"),
        P(),
        P(),
        P("lon", ("groups", "lat"), None),
        P("lon", ("groups", "lat"), None),
        P("lon", ("groups", "lat")),
    )
    out_specs = (P(None, ("groups", "lat"), "lon"), P(None, ("groups", "lat"), "lon"))
    return jax.shard_map(
        functools.partial(body, mesh.shape["lat"] // 2),
        mesh=mesh,
        in_specs=in_specs,
        out_specs=out_specs,
        check_vma=False,
    )
```

```python
import functools

import jax
import jax.numpy as jnp
from jax import lax
from jax.experimental import pallas as pl
from jax.experimental.pallas import tpu as pltpu
from jax.sharding import PartitionSpec as P

HALF = 32
TAPS = 2 * HALF + 1
LOWER = 0.25
UPPER = 120.0
THETA = (LOWER + UPPER) / 2.0
DELTA = (UPPER - LOWER) / 2.0
SIGMA = THETA / DELTA
RHO = 1.0 / SIGMA
NEW_RHO = 1.0 / (2.0 * SIGMA - RHO)
BLOCK = 256
EDGE = 128
LEFT_COST = 5 * 10**9
ADJOINT_COST = 2 * 10**10
PACK_VMEM = 62 * 2**20
AXES = ("lat", "lon")

VMEM = pl.BlockSpec(memory_space=pltpu.VMEM)
SMEM = pl.BlockSpec(memory_space=pltpu.SMEM)
HBM = pl.BlockSpec(memory_space=pltpu.HBM)
F32 = jnp.float32
BF16 = jnp.bfloat16


def place():
    lat = lax.axis_index("lat")
    return lat // 2, lax.rem(lat, 2), lax.axis_index("lon")


def open_sides(pairs):
    k, y, _ = place()
    north, south = jnp.where(k == 0, 0.0, 1.0), jnp.where(k == pairs - 1, 0.0, 1.0)
    flip = lax.rem(k + y, 2) == 1
    return jnp.where(flip, north, south), jnp.where(flip, south, north)


def lead_trail(own, pair):
    k, y, _ = place()
    straight = lax.rem(k, 2) == 1
    return jnp.where(straight, own, pair), jnp.where(straight, pair, own)


def shape(*dims, dtype=F32):
    return jax.ShapeDtypeStruct(dims, dtype)


def call(
    kernel, out_shape, args, specs=None, outs=None, scratch=(), flops=0, vmem=24 * 2**20, aliases=None, name=None
):
    nbytes = 0 if flops == 0 else sum(a.size * a.dtype.itemsize for a in args)
    return list(pl.pallas_call(
        kernel,
        out_shape=out_shape,
        in_specs=specs or [VMEM] * len(args),
        out_specs=outs or [VMEM] * len(out_shape),
        scratch_shapes=list(scratch),
        input_output_aliases=aliases or {},
        compiler_params=pltpu.CompilerParams(vmem_limit_bytes=vmem),
        cost_estimate=pl.CostEstimate(flops=flops, bytes_accessed=nbytes, transcendentals=0),
        name=name,
    )(*args))


def pack_kernel(own, guess_ref, land_ref, coef_ref, first_ref, second_ref, *scratch):
    guess, land, coef, packed, sems = scratch
    _, y, c = place()
    row = y if own else 1 - y
    days = (2 * c + row, 2 * (1 - c) + row)
    rows, width = land.shape
    start = pl.multiple_of((rows - 8) * y, 8)
    copies = [
        pltpu.make_async_copy(land_ref, land, sems.at[0]),
        pltpu.make_async_copy(coef_ref.at[pl.ds(start, 8), :], coef, sems.at[1]),
    ]
    for i, day in enumerate(days):
        copies.append(pltpu.make_async_copy(guess_ref.at[day], guess.at[i], sems.at[2 + i]))
    for copy in copies:
        copy.start()
    copies[0].wait()
    copies[1].wait()
    edge = jnp.where(y == 0, coef[:1, :], coef[7:, :])
    edge = jnp.concatenate([edge[:, i : i + 128] for i in range(0, width, 128)], axis=0)
    outs = []
    for i, ref in enumerate((first_ref, second_ref)):
        copies[2 + i].wait()
        for group in range(rows // 8):
            part = slice(8 * group, 8 * group + 8)
            sea = land[part, :].astype(F32)
            packed[i, :, width * group : width * (group + 1)] = guess[i, part, :] * sea
        packed[i, :, width * (rows // 8) :] = edge
        outs.append(pltpu.make_async_copy(packed.at[i], ref, sems.at[4 + i]))
        outs[-1].start()
    for out in outs:
        out.wait()


def order_kernel(own_ref, pair_ref, diag_ref, core_ref, lead_ref, trail_ref):
    size = own_ref.shape[1]
    for i, (own, pair) in enumerate(((own_ref, pair_ref), (core_ref, diag_ref))):
        lead, trail = lead_trail(own[...], pair[...])
        lead_ref[:, size * i : size * (i + 1)] = lead
        trail_ref[:, size * i : size * (i + 1)] = trail


def obs_kernel(obs_ref, precision_ref, counts_ref, keep_ref, send_ref):
    _, y, c = place()
    width = obs_ref.shape[2] // 2
    for day, ref in ((y, keep_ref), (1 - y, send_ref)):
        counts = counts_ref[day].astype(F32)
        for half, side in ((0, c), (1, 1 - c)):
            source = pl.ds(pl.multiple_of(side * width, width), width)
            target = pl.ds(half * width, width)
            ref[0, :, target] = obs_ref[day, :, source].astype(F32)
            ref[1, :, target] = counts * precision_ref[day, :, source].astype(F32)


def split(values):
    high = values.astype(BF16)
    return high, (values - high.astype(F32)).astype(BF16)


def banded(kern_ref, offset):
    forward = jnp.zeros(offset.shape, F32)
    adjoint = jnp.zeros(offset.shape, F32)
    for tap in range(TAPS):
        hit = offset == tap
        forward = jnp.where(hit, kern_ref[tap], forward)
        adjoint = jnp.where(hit, kern_ref[TAPS - 1 - tap], adjoint)
    return forward, adjoint


def matrix_kernel(pairs, rows, lat_ref, lon_ref, lat_fwd_ref, lat_adj_ref, lon_fwd_ref, lon_adj_ref):
    k, y, _ = place()
    dims = (2 * rows, 4 * rows)

    flip = lax.rem(k + y, 2) == 1
    out = lax.broadcasted_iota(jnp.int32, dims, 0)
    col = lax.broadcasted_iota(jnp.int32, dims, 1)
    target = rows * jnp.where(y == 0, out // rows, 1 - out // rows) + out % rows
    source = rows * jnp.where(flip, col // rows - 1, 2 - col // rows) + col % rows
    offset = source - target + HALF
    lead_open, trail_open = open_sides(pairs)
    inside = jnp.where(col < 3 * rows, 1.0, trail_open)
    inside = jnp.where(col < rows, lead_open, inside)
    for ref, matrix in zip((lat_fwd_ref, lat_adj_ref), banded(lat_ref, offset)):
        high, low = split(matrix * inside)
        ref[: 2 * rows, : 4 * rows] = high
        ref[: 2 * rows, 4 * rows :] = high
        ref[2 * rows :, : 4 * rows] = low
        ref[2 * rows :, 4 * rows :] = jnp.zeros(dims, BF16)
    dims = (EDGE, EDGE)
    offset = lax.broadcasted_iota(jnp.int32, dims, 0) - lax.broadcasted_iota(jnp.int32, dims, 1)
    for ref in (lon_fwd_ref, lon_adj_ref):
        ref[...] = jnp.zeros(ref.shape, BF16)
    for distance in range(3):
        pair = banded(lon_ref, offset + EDGE * distance - (EDGE - HALF))
        for ref, matrix in zip((lon_fwd_ref, lon_adj_ref), pair):
            for part, piece in enumerate(split(matrix)):
                for column in range(BLOCK // EDGE):
                    row = EDGE * (column + distance)
                    ref[part, row : row + EDGE, EDGE * column : EDGE * (column + 1)] = piece


def load(ref):
    if ref.shape[0] > 8:
        return ref[...]
    size, groups = ref.shape[1] // 2, HALF // 8
    width = (size - 128) // groups
    return jnp.concatenate(
        [
            jnp.concatenate(
                [ref[:, size * half + width * i : size * half + width * (i + 1)] for half in range(2)],
                axis=1,
            )
            for i in range(groups)
        ],
        axis=0,
    )


def edge_row(ref):
    size = ref.shape[1] // 2
    tiles = [ref[:, size * half - 128 : size * half] for half in (1, 2)]
    return jnp.concatenate([tile[i : i + 1, :] for tile in tiles for i in range(8)], axis=1)


def lat_conv(blocks, matrix_ref):
    high, low = split(jnp.concatenate(blocks, axis=0))
    stacked = jnp.concatenate([high, low], axis=0)
    both = jnp.dot(matrix_ref[...], stacked, preferred_element_type=F32)
    half = both.shape[0] // 2
    return both[:half] + both[half:]


def lon_conv(field, matrix_ref):
    rows, length = field.shape
    count = length // BLOCK
    parts = []
    for part in split(field):
        wide = jnp.concatenate([part[:, -EDGE:], part, part[:, :EDGE]], axis=1)
        parts += [wide[:, BLOCK * i : BLOCK * (i + 1) + 2 * EDGE] for i in range(count)]
    coarse = jnp.dot(jnp.concatenate(parts, axis=0), matrix_ref[0], preferred_element_type=F32)
    fine = jnp.dot(
        jnp.concatenate(parts[:count], axis=0), matrix_ref[1], preferred_element_type=F32
    )
    out = coarse[: count * rows] + coarse[count * rows :] + fine
    return jnp.concatenate([out[rows * i : rows * (i + 1)] for i in range(count)], axis=1)


def seen_kernel(*refs):
    lat_ref, fwd_ref, seen_ref = refs[4:]
    seen_ref[...] = lon_conv(lat_conv([load(ref) for ref in refs[:4]], lat_ref), fwd_ref)


def misfit_kernel(seen_ref, keep_ref, sent_ref, adj_ref, *outs):
    obs = jnp.concatenate([keep_ref[0], sent_ref[0]], axis=0)
    weight = jnp.concatenate([keep_ref[1], sent_ref[1]], axis=0)
    spread = lon_conv(weight * (obs - seen_ref[...]), adj_ref)
    rows, width = outs[0].shape
    lead, trail = lead_trail(spread[:rows], spread[rows:])
    for part, (lead_ref, trail_ref) in enumerate(zip(outs[::2], outs[1::2])):
        columns = slice(width * part, width * (part + 1))
        lead_ref[...] = lead[:, columns]
        trail_ref[...] = trail[:, columns]


def beside(center, above, below):
    width = center.shape[1]
    lateral = pltpu.roll(center, 1, 1) + pltpu.roll(center, width - 1, 1)
    return above + below + lateral


def rim(ref, last):
    if ref.shape[0] > 8:
        return ref[ref.shape[0] - 8 :, :] if last else ref[:8, :]
    size, groups = ref.shape[1] // 2, HALF // 8
    width = (size - 128) // groups
    start = width * (groups - 1) if last else 0
    return jnp.concatenate(
        [ref[:, size * half + start : size * half + start + width] for half in range(2)], axis=1
    )


def prior_kernel(pairs, *refs):
    lead_ref, trail_ref = refs[0], refs[3]
    inside = [load(ref) for ref in refs[1:3]]
    lead_edge, trail_edge = edge_row(refs[4]), edge_row(refs[5])
    out_ref, ext, wide, inner = refs[10:]
    k, y, _ = place()
    rows, length = inside[0].shape
    flip = lax.rem(k + y, 2) == 1
    north_open = jnp.where(k == 0, 0.0, 1.0)
    south_open = jnp.where(k == pairs - 1, 0.0, 1.0)
    for block, field in enumerate(inside):
        where = 16 + rows * jnp.where(flip, block, 1 - block)
        ext[pl.ds(pl.multiple_of(where, 8), rows), :] = field
    north = jnp.where(flip, rim(lead_ref, True), rim(trail_ref, True))
    south = jnp.where(flip, rim(trail_ref, False), rim(lead_ref, False))
    ext[8:16, :] = north * north_open
    ext[16 + 2 * rows : 24 + 2 * rows, :] = south * south_open
    for block, (left, right) in enumerate(map_pairs(refs[6:10])):
        where = pl.multiple_of(8 + rows * jnp.where(y == 0, block, 1 - block), 8)
        coef = jnp.concatenate([left[0], right[0]], axis=1) + 4.0
        wide[pl.ds(where, rows), :] = coef
    north = jnp.where(flip, lead_edge, trail_edge) + 4.0
    south = jnp.where(flip, trail_edge, lead_edge) + 4.0
    wide[:8, :] = jnp.broadcast_to(north, (8, length))
    wide[8 + 2 * rows :, :] = jnp.broadcast_to(south, (8, length))
    count = 2 * rows + 16
    ext[:8, :] = jnp.zeros((8, length), F32)
    ext[8 + count :, :] = jnp.zeros((8, length), F32)
    center = ext[8 : 8 + count, :]
    around = beside(center, ext[7 : 7 + count, :], ext[9 : 9 + count, :])
    inner[...] = wide[...] * center - around
    inner[:8, :] = inner[:8, :] * north_open
    inner[8 + 2 * rows :, :] = inner[8 + 2 * rows :, :] * south_open
    center = inner[8 : 8 + 2 * rows, :]
    around = beside(center, inner[7 : 7 + 2 * rows, :], inner[9 : 9 + 2 * rows, :])
    outer = wide[8 : 8 + 2 * rows, :] * center - around
    top, bottom = outer[:rows], outer[rows:]
    out_ref[:rows, :] = jnp.where(y == 0, top, bottom)
    out_ref[rows:, :] = jnp.where(y == 0, bottom, top)


def map_pairs(refs):
    return refs[:2], refs[2:]


def adjoint_kernel(*refs):
    refs[5][...] = lat_conv([ref[...] for ref in refs[:4]], refs[4])


def update_kernel(back_ref, prior_ref, *refs):
    rows, width = back_ref.shape[0] // 2, back_ref.shape[1] // 2
    last = back_ref[...] - prior_ref[...]
    sea = [jnp.concatenate([left[1], right[1]], axis=1) for left, right in map_pairs(refs[:4])]
    last_own, last_pair = last[:rows] * sea[0], last[rows:] * sea[1]
    base, states, outs = refs[4:6], refs[6:8], refs[8:]
    for before, state, change in zip(base, states, lead_trail(last_own, last_pair)):
        state[...] = load(before) + change * (1.0 / THETA)
    for i in range(2):
        outs[2 * i][...] = last_own[:, width * i : width * (i + 1)]
        outs[2 * i + 1][...] = last_pair[:, width * i : width * (i + 1)]


def last_kernel(half, *refs):
    lat_ref, prior_ref = refs[4:6]
    rows, width = refs[0].shape
    last = lat_conv([ref[...] for ref in refs[:4]], lat_ref)
    last = last - prior_ref[:, width * half : width * (half + 1)]
    own, pair = map_pairs(refs[6:10])
    refs[10][...] = last[:rows] * own[half][1]
    refs[11][...] = last[rows:] * pair[half][1]


def days_of():
    _, y, c = place()
    return 2 * c + y, 2 * c + (1 - y), 2 * (1 - c) + (1 - y), 2 * (1 - c) + y


def early_kernel(*refs):
    guess_ref, land_ref, fixed_ref, state_ref = refs[4:]
    land = 1.0 - land_ref[...].astype(F32)
    for i, (day, ref) in enumerate(zip(days_of(), refs[:4])):
        guess = guess_ref[day]
        update = (ref[...] - land * guess) * (1.0 / THETA)
        state = guess + update
        fixed_ref[i] = land * state
        state_ref[i] = state + (NEW_RHO * RHO) * update


def final_kernel(half, *refs):
    late, (fixed_ref, sum_ref) = refs[:2], refs[2:4]
    state_ref, last_ref, state, last, sems = refs[-5:]
    days = days_of()[2 * half : 2 * half + 2]
    copies = []
    for i, (day, ref) in enumerate(zip(days, late)):
        last[i] = ref[...] - fixed_ref[2 * half + i]
        state[i] = sum_ref[2 * half + i] + (2.0 * NEW_RHO / DELTA) * last[i]
        for j, (source, target) in enumerate(((state, state_ref), (last, last_ref))):
            copies.append(pltpu.make_async_copy(source.at[i], target.at[day], sems.at[2 * i + j]))
            copies[-1].start()
    for copy in copies:
        copy.wait()


def body(
    pairs,
    first_guess,
    range_coef,
    land_sea,
    lat_kernel,
    lon_kernel,
    observations,
    obs_precision,
    track_counts,
):
    days, rows, width = first_guess.shape
    length = observations.shape[2]
    assert days == 4 and rows == HALF and length == 2 * width and length % BLOCK == 0
    assert width == 8 * 128
    places = [(k, y, c) for k in range(pairs) for y in range(2) for c in range(2)]

    def permute(array, move):
        moves = [(i, places.index(move(*at))) for i, at in enumerate(places)]
        return lax.ppermute(array, AXES, moves)

    def swap(k, y, c, parity):
        target = k + 1 if (k + y) % 2 == parity else k - 1
        return (target, y, c) if 0 <= target < pairs else (k, y, 1 - c)

    core = lambda array: permute(array, lambda k, y, c: (k, y, 1 - c))
    pair = lambda array: permute(array, lambda k, y, c: (k, 1 - y, c))
    diag = lambda array: permute(array, lambda k, y, c: (k, 1 - y, 1 - c))
    lead = lambda array: permute(array, lambda k, y, c: swap(k, y, c, 0))
    trail = lambda array: permute(array, lambda k, y, c: swap(k, y, c, 1))

    piece = shape(rows, width)
    packed = shape(8, rows // 8 * width + 128)
    def pack(is_own, land):
        return call(
            functools.partial(pack_kernel, is_own),
            [packed] * 2,
            [first_guess, land, range_coef],
            [HBM] * 3,
            outs=[HBM] * 2,
            scratch=[
                pltpu.VMEM((2, rows, width), F32),
                pltpu.VMEM((rows, width), jnp.int32),
                pltpu.VMEM((8, width), F32),
                pltpu.VMEM((2,) + packed.shape, F32),
                pltpu.SemaphoreType.DMA((6,)),
            ],
            vmem=PACK_VMEM,
            name="pack",
        )

    to_pair, to_diag = pack(False, land_sea)
    land, to_pair = lax.optimization_barrier((land_sea, to_pair))
    own, to_core = pack(True, land)
    by_pair, by_diag = pair(to_pair), diag(to_diag)
    observations, own = lax.optimization_barrier((observations, own))
    by_core = core(to_core)
    keep, send = call(
        obs_kernel,
        [shape(2, rows, length)] * 2,
        [observations, obs_precision, track_counts[:, :, None]],
        name="observed",
    )
    maps = jnp.stack([range_coef, land_sea.astype(F32)])
    sent = pair(send)
    v_lead, v_trail = call(
        order_kernel,
        [shape(8, 2 * packed.shape[1])] * 2,
        [own, by_pair, by_diag, by_core],
        flops=ADJOINT_COST,
        name="order",
    )
    maps, lat_kernel, v_lead = lax.optimization_barrier((maps, lat_kernel, v_lead))
    lat_fwd, lat_adj, lon_fwd, lon_adj = call(
        functools.partial(matrix_kernel, pairs, rows),
        [shape(4 * rows, 8 * rows, dtype=BF16)] * 2
        + [shape(2, BLOCK + 2 * EDGE, BLOCK, dtype=BF16)] * 2,
        [lat_kernel, lon_kernel],
        [SMEM, SMEM],
        flops=4 * 65 * 2 * 70000,
        name="matrices",
    )
    fields = [lead(v_lead), v_lead, v_trail, trail(v_trail)]
    by_lon = core(maps)
    fields[0], by_lon = lax.optimization_barrier((fields[0], by_lon))
    edges = [fields[0], fields[3]]
    band = shape(rows, length)
    conv = 2 * 3 * 2 * rows * length * 512
    for step in range(2):
        (seen,) = call(
            seen_kernel,
            [shape(2 * rows, length)],
            fields + [lat_fwd, lon_fwd],
            flops=2 * conv,
            name="seen",
        )
        misfit = call(
            misfit_kernel,
            [piece] * 4 if step else [band] * 2,
            [seen, keep, sent, lon_adj],
            flops=conv,
            name="misfit",
        )
        if not step:
            maps, misfit[0] = lax.optimization_barrier((maps, misfit[0]))
            maps_pair = pair(maps)
            maps = [maps, by_lon, maps_pair, core(maps_pair)]
        (prior,) = call(
            functools.partial(prior_kernel, pairs),
            [shape(2 * rows, length)],
            fields + edges + maps,
            scratch=[
                pltpu.VMEM((2 * rows + 32, length), F32),
                pltpu.VMEM((2 * rows + 16, length), F32),
                pltpu.VMEM((2 * rows + 16, length), F32),
            ],
            name="prior",
        )
        common = [lat_adj, prior] + maps
        moved = [lead(m) if i % 2 == 0 else trail(m) for i, m in enumerate(misfit)]
        if not step:
            (back,) = call(
                adjoint_kernel,
                [shape(2 * rows, length)],
                [moved[0], *misfit, moved[1], lat_adj],
                flops=ADJOINT_COST,
                name="adjoint",
            )
            v_lead, v_trail, *pieces = call(
                update_kernel,
                [band] * 2 + [piece] * 4,
                [back, prior, *maps, v_lead, v_trail],
                name="update",
            )
            fields = [lead(v_lead), v_lead, v_trail, trail(v_trail)]
            pieces = [pieces[0], pair(pieces[1]), diag(pieces[3]), core(pieces[2])]
            early = call(
                early_kernel,
                [shape(days, rows, width)] * 2,
                pieces + [first_guess, land_sea],
                name="early",
            )
    moved[0], *early = lax.optimization_barrier((moved[0], *early))
    left_own, left_pair = call(
        functools.partial(last_kernel, 0),
        [piece] * 2,
        [moved[0], *misfit[:2], moved[1], *common],
        flops=LEFT_COST,
        name="update",
    )
    right_own, right_pair = call(
        functools.partial(last_kernel, 1),
        [piece] * 2,
        [moved[2], *misfit[2:], moved[3], *common],
        flops=conv,
        name="update",
    )
    pieces = [left_own, pair(left_pair), diag(right_pair), core(right_own)]
    result = []
    for half in range(2):
        args = pieces[2 * half : 2 * half + 2] + early
        result = call(
            functools.partial(final_kernel, half),
            [shape(days, rows, width)] * 2,
            args + (result if half else []),
            [VMEM] * 4 + [HBM] * 2 * half,
            outs=[HBM] * 2,
            scratch=[
                pltpu.VMEM((2, rows, width), F32),
                pltpu.VMEM((2, rows, width), F32),
                pltpu.SemaphoreType.DMA((4,)),
            ],
            aliases={4: 0, 5: 1} if half else {},
            flops=0 if half else LEFT_COST,
            name="final",
        )
    return tuple(result)


def solution(mesh):
    assert mesh.shape["lat"] % 2 == 0 and mesh.shape["lon"] == 2
    in_specs = (
        P(None, ("groups", "lat"), "lon"),
        P(("groups", "lat"), "lon"),
        P(("groups", "lat"), "lon"),
        P(),
        P(),
        P("lon", ("groups", "lat"), None),
        P("lon", ("groups", "lat"), None),
        P("lon", ("groups", "lat")),
    )
    out_specs = (P(None, ("groups", "lat"), "lon"), P(None, ("groups", "lat"), "lon"))
    return jax.shard_map(
        functools.partial(body, mesh.shape["lat"] // 2),
        mesh=mesh,
        in_specs=in_specs,
        out_specs=out_specs,
        check_vma=False,
    )
```
